32 devices in a mesh: blk: 16 (over z, y, core), grp: 2 (over x).
Axes of the slice: x: 2, y: 2, z: 4, core: 2. Of those that a mesh axis runs over, the one named last changes fastest.
Arguments:
- features: bfloat16 [2, 16384, 2048], P('grp', 'blk'), may hold values from -6 to 6
- neighbours: int32 [2, 16384, 64], P('grp', 'blk'), may hold values from 0 to 1535
- degree: int32 [2, 16384], P('grp', 'blk'), may hold values from 16 to 64, as said below
- weight_one: bfloat16 [2048, 2048], replicated, may hold values from -0.5 to 0.5
- bias_one: float32 [2048], replicated, may hold values from -3 to 3
- weight_two: bfloat16 [2048, 2048], replicated, may hold values from -0.5 to 0.5
- bias_two: float32 [2048], replicated, may hold values from -3 to 3
- cotangent: bfloat16 [2, 16384, 2048], P('grp', 'blk'), may hold values from -6 to 6
Outputs:
- activations: bfloat16 [2, 16384, 2048], P('grp', 'blk')
- input_grad: bfloat16 [2, 16384, 2048], P('grp', 'blk')
- grad_weight_one: float32 [2048, 2048], P(('blk', 'grp'))
- grad_bias_one: float32 [2048], P(('blk', 'grp'))
- grad_weight_two: float32 [2048, 2048], P(('blk', 'grp'))
- grad_bias_two: float32 [2048], P(('blk', 'grp'))
The draws below stay inside these ranges and needn't reach their ends.
Inputs may be any that keep to these rules, and one draw needn't show every extreme that they name: `degree`: used slots of a node's neighbour list; in each block of 1024 nodes some node uses all 64. `neighbours`: rows of the node's window: the last 256 nodes of the previous block, the 1024 nodes of its own, then the first 256 of the next; unused slots hold arbitrary rows.
All inputs are finite; a program needn't handle non-finite values.
Results may differ from the reference program's by a relative error of at most 0.013.
Values may be sent and summed in bfloat16 or wider, within the bound.
No kernel may reach another device: no remote copies, remote signals or barrier semaphores. Data moves between devices by JAX's collectives and lax.ppermute only.
A program may use at most 192 MiB of HBM per device.

```python
import jax
import jax.numpy as jnp
from jax import lax

D = 2048
NODE_DEV = 1024
MAXDEG = 64
BAND = 256
CYCLE = 16384
GROUPS = 2
N_BLK = 16


def draw_degree(key, part):
    key = jax.random.fold_in(key, 7)
    key_base, key_flag, key_hub, key_rate, key_full = jax.random.split(key, 5)
    base_deg = jax.random.randint(key_base, (GROUPS, CYCLE), MAXDEG // 4, 3 * MAXDEG // 4 + 1)
    hub_deg = jax.random.randint(key_hub, (GROUPS, CYCLE), 3 * MAXDEG // 4, MAXDEG + 1)
    hub_rate = jnp.repeat(jax.random.randint(key_rate, (GROUPS, N_BLK), 0, 3), NODE_DEV, axis=1)
    hub_flag = jax.random.randint(key_flag, (GROUPS, CYCLE), 0, 8) <= hub_rate
    chosen = jnp.repeat(jax.random.randint(key_full, (GROUPS, N_BLK), 0, NODE_DEV), NODE_DEV, axis=1)
    position = jnp.arange(CYCLE, dtype=jnp.int32) % NODE_DEV
    full_row = position[None, :] == chosen
    result = jnp.where(hub_flag, hub_deg, base_deg)
    return jnp.where(full_row, MAXDEG, result).astype(jnp.int32)


def touch_ends(entries, stream_key, low, high):
    extent = entries.shape
    spot = [jax.random.randint(jax.random.fold_in(stream_key, axis), (), 0, extent[axis]) for axis in range(len(extent))]
    entries = entries.at[tuple(spot)].set(low)
    longest = extent.index(max(extent))
    spot[longest] = (spot[longest] + 1) % extent[longest]
    return entries.at[tuple(spot)].set(high)


def spiked(values, own_key, source, target, shards_of, factor):
    owner, partner = [(jnp.arange(values.shape[dim]) // (values.shape[dim] // shards_of)).reshape([-1 if axis == dim else 1 for axis in range(values.ndim)]) for dim in (source, target)]
    chosen = jax.random.permutation(own_key, shards_of)[partner]
    strong = (owner == chosen) | (owner == (partner + shards_of // 2) % shards_of)
    return jnp.where(strong, factor * values, values)


def block_levels(key, shape, pieces, smallest, largest):
    def one(axis_at, parts):
        heights = jax.random.uniform(jax.random.fold_in(jax.random.fold_in(key, 6), axis_at), (parts,), jnp.float32, smallest / len(pieces), largest / len(pieces))
        return jnp.repeat(jnp.exp(heights), shape[axis_at] // parts).reshape((-1,) + (1,) * (len(shape) - axis_at - 1))

    factor_of = one(*pieces[0])
    for cut in pieces[1:]:
        factor_of = factor_of * one(*cut)
    return factor_of


def centred(rng, extent, width, most, cuts=(), kind=jnp.bfloat16):
    factor_of = block_levels(rng, extent, cuts, -0.22, 0.18) if cuts else 1.0
    array = jax.random.normal(rng, extent, jnp.float32) * width * factor_of
    return jnp.minimum(jnp.maximum(array, -most), most).astype(kind)


def heavy_noise(rng, shape, width, reach, shards, heavy, kind=jnp.bfloat16):
    values = width * jax.random.normal(rng, shape, jnp.float32)
    if shards:
        values = values * block_levels(rng, shape, shards, -0.22, 0.18)
    return jnp.clip(spiked(values, jax.random.fold_in(rng, 3), *heavy), -reach, reach).astype(kind)


def setup_inputs(seed: int = 0) -> dict:
    key_list = jax.random.split(jax.random.key(seed), 9)
    return {
        "features": heavy_noise(key_list[0], (GROUPS, CYCLE, D), 1.0, 6.0, ((0, 2), (1, 16)), (1, 2, 16, 2.0)),
        "neighbours": touch_ends(jax.random.randint(key_list[1], (GROUPS, CYCLE, MAXDEG), 0, NODE_DEV + 2 * BAND), jax.random.fold_in(key_list[1], 1), 0, (NODE_DEV + 2 * BAND) - 1).astype(jnp.int32),
        "degree": draw_degree(jax.random.fold_in(key_list[8], 71), 0),
        "weight_one": centred(key_list[3], (D, D), (D // 16) ** -0.5, 0.5),
        "bias_one": centred(key_list[4], (D,), 0.5, 3.0, (), jnp.float32),
        "weight_two": centred(key_list[5], (D, D), (D // 16) ** -0.5, 0.5),
        "bias_two": centred(key_list[6], (D,), 0.5, 3.0, (), jnp.float32),
        "cotangent": centred(key_list[7], (GROUPS, CYCLE, D), 1.0, 6.0, ((0, 2), (1, 16))),
    }


@jax.custom_vjp
def low(v):
    return lax.optimization_barrier(v.astype(jnp.bfloat16)).astype(jnp.float32)

@jax.custom_vjp
def low_back(v):
    return v

def low_keep(v):
    return (low(v), None)

def low_pass(kept, grad):
    return (grad,)

def back_keep(v):
    return (v, None)

def back_low(kept, grad):
    return (low(grad),)
low.defvjp(low_keep, low_pass)
low_back.defvjp(back_keep, back_low)

def make_window(inputs):
    blocks = inputs.reshape(GROUPS, N_BLK, NODE_DEV, D)
    before = jnp.roll(blocks, 1, axis=1)[:, :, NODE_DEV - BAND:]
    following = jnp.roll(blocks, -1, axis=1)[:, :, :BAND]
    joined = jnp.concatenate([before, blocks, following], axis=2)
    return joined.reshape(GROUPS * N_BLK, NODE_DEV + 2 * BAND, D)

def block_sum(operands):
    window, slots, slot_used = operands
    return lax.optimization_barrier(jnp.sum(window[slots] * slot_used[:, :, None], axis=1))

def gcn_layer(inputs, weight, bias_vec, neighbours, degree):
    window = make_window(inputs)
    slots = neighbours.reshape(GROUPS * N_BLK, NODE_DEV, MAXDEG).astype(jnp.int32)
    slot_ids = jnp.arange(MAXDEG, dtype=jnp.int32)
    slot_used = (slot_ids[None, None, :] < degree[:, :, None]).astype(jnp.float32)
    slot_used = slot_used.reshape(GROUPS * N_BLK, NODE_DEV, MAXDEG)
    neighbour_sum = lax.map(jax.checkpoint(block_sum), (window, slots, slot_used))
    neighbour_sum = neighbour_sum.reshape(GROUPS, CYCLE, D)
    pre_sum = low_back(neighbour_sum + 2.0 * inputs)
    averaged = low(pre_sum / (degree[:, :, None].astype(jnp.float32) + 1.0))
    preact = low_back(jnp.dot(averaged, weight, precision=lax.Precision.HIGHEST) + bias_vec)
    return jax.nn.gelu(preact)

def reference(features, neighbours, degree, weight_one, bias_one, weight_two, bias_two, cotangent):

    def forward(inputs, first_w, first_b, second_w, second_b):
        hidden = low(gcn_layer(inputs, first_w, first_b, neighbours, degree))
        return gcn_layer(hidden, second_w, second_b, neighbours, degree)
    output, pullback = jax.vjp(forward, features.astype(jnp.float32), weight_one.astype(jnp.float32), bias_one, weight_two.astype(jnp.float32), bias_two)
    gradients = pullback(cotangent.astype(jnp.float32))
    return (output.astype(jnp.bfloat16), gradients[0].astype(jnp.bfloat16), gradients[1], gradients[2], gradients[3], gradients[4])
```

```python
import jax
import jax.numpy as jnp
from jax import lax
from jax.experimental import pallas as pl
from jax.experimental.pallas import tpu as pltpu
from jax.sharding import PartitionSpec as P

BAND = 256
BF = jnp.bfloat16
F32 = jnp.float32


def count_kernel(slots_ref, degree_ref, out_ref):
    slot_total, lanes = slots_ref.shape
    width = out_ref.shape[0]
    quarter = width // 4
    parts = 2
    rows = quarter // parts
    degree = degree_ref[...]
    block = pl.program_id(0)
    node = lax.broadcasted_iota(jnp.int32, (rows, lanes), 1) + block * lanes
    sub = lax.broadcasted_iota(jnp.int32, (rows, lanes), 0)
    for part in range(parts):
        ids = sub + part * rows

        def add_slot(k, packed):
            slot = slots_ref[pl.ds(k, 1), :]
            q = (
                (slot >= quarter).astype(jnp.int32)
                + (slot >= 2 * quarter).astype(jnp.int32)
                + (slot >= 3 * quarter).astype(jnp.int32)
            )
            key = slot - q * quarter
            value = jnp.where(k < degree, jnp.left_shift(1, q * 8), 0)
            return packed + jnp.where(ids == key, value, 0)

        packed = lax.fori_loop(
            0, slot_total, add_slot, jnp.zeros((rows, lanes), jnp.int32), unroll=4
        )
        for q in range(4):
            count = jnp.bitwise_and(jnp.right_shift(packed, 8 * q), 255)
            own = ids + (q * quarter - BAND) == node
            count = count + jnp.where(own, 2, 0)
            out_ref[pl.ds(q * quarter + part * rows, rows), :] = count.astype(F32).astype(BF)


def count_table(slots, degree):
    nodes, slot_total = slots.shape
    width = nodes + 2 * BAND
    return pl.pallas_call(
        count_kernel,
        grid=(nodes // 128,),
        in_specs=[
            pl.BlockSpec((slot_total, 128), lambda i: (0, i)),
            pl.BlockSpec((1, 128), lambda i: (0, i)),
        ],
        out_specs=pl.BlockSpec((width, 128), lambda i: (0, i)),
        out_shape=jax.ShapeDtypeStruct((width, nodes), BF),
        cost_estimate=pl.CostEstimate(flops=0, bytes_accessed=4 << 20, transcendentals=0),
    )(slots.T, degree[None, :])


def dot(a, b, contract):
    return lax.dot_general(a, b, (contract, ((), ())), preferred_element_type=F32)


def halo(field):
    count = lax.axis_size("blk")
    nodes = field.shape[0]
    before = lax.ppermute(field[nodes - BAND :], "blk", [(i, (i + 1) % count) for i in range(count)])
    after = lax.ppermute(field[:BAND], "blk", [((i + 1) % count, i) for i in range(count)])
    return before, after


def aggregate(field, table, degree_plus, weight, bias_vec):
    before, after = halo(field)
    window = jnp.concatenate([before, field, after], axis=0)
    pre_sum = dot(table, window, ((0,), (0,)))
    averaged = (pre_sum / degree_plus).astype(BF)
    preact = dot(averaged, weight, ((1,), (0,))) + bias_vec
    return averaged, preact


def swap_half(total, dim, bit, partner, axis):
    size = total.shape[dim] // 2
    send = lax.dynamic_slice_in_dim(total, (1 - bit) * size, size, dim)
    keep = lax.dynamic_slice_in_dim(total, bit * size, size, dim)
    received = lax.ppermute(send.astype(BF), axis, partner)
    return keep + received.astype(F32)


def line_sum(total, place, count, step_perm):
    mine = lax.dynamic_index_in_dim(total, place, 0, keepdims=False)
    below = None
    above = None
    for step in range(1, count):
        def part(index, carried):
            chunk = lax.dynamic_index_in_dim(total, jnp.clip(index, 0, count - 1), 0, keepdims=False)
            return chunk if carried is None else chunk + carried.astype(F32)

        up = part(place + count - step, below).astype(BF)
        down = part(place - count + step, above).astype(BF)
        below = lax.ppermute(up, "blk", step_perm([(z, z + 1) for z in range(step)]))
        above = lax.ppermute(
            down, "blk", step_perm([(z, z - 1) for z in range(count - step, count)])
        )
    return mine + below.astype(F32) + above.astype(F32)


def scatter_sum(averaged, grad_pre):
    blk, grp = lax.axis_size("blk"), lax.axis_size("grp")
    b, g = lax.axis_index("blk"), lax.axis_index("grp")
    core, y, z = b % 2, (b // 2) % 2, b // 4
    line = blk // 4
    nodes, width = averaged.shape
    rows = width // (blk * grp)

    def step_perm(pairs):
        return [(4 * s + r, 4 * t + r) for s, t in pairs for r in range(4)]

    by_core = averaged.reshape(nodes, blk // 2, 2, grp * rows)

    def half(which):
        return lax.dynamic_index_in_dim(by_core, which, 2, keepdims=False).reshape(nodes, width // 2)

    send = dot(half(1 - core), grad_pre, ((0,), (0,))).astype(BF)
    received = lax.ppermute(send, "blk", [(i, i ^ 1) for i in range(blk)])
    total = dot(half(core), grad_pre, ((0,), (0,))) + received.astype(F32)
    total = total.reshape(line, 2, grp, rows, width)
    span = grp
    while span > 1:
        span //= 2
        total = swap_half(total, 2, (g // span) % 2, [(i, i ^ span) for i in range(grp)], "grp")
    total = total[:, :, 0]
    total = line_sum(total, z, line, step_perm)
    total = swap_half(total, 0, y, [(i, i ^ 2) for i in range(blk)], "blk")
    return total[0]


def layer_back(grad_out, preact, averaged, table, degree_plus, weight):
    nodes = averaged.shape[0]
    blk = lax.axis_size("blk")
    _, gelu_pull = jax.vjp(jax.nn.gelu, preact)
    grad_pre = gelu_pull(grad_out)[0].astype(BF)
    grad_weight = scatter_sum(averaged, grad_pre)
    grad_bias = lax.psum_scatter(
        jnp.sum(grad_pre.astype(F32), axis=0), ("blk", "grp"), scatter_dimension=0, tiled=True
    )
    grad_avg = dot(grad_pre, weight, ((1,), (1,)))
    grad_scaled = (grad_avg / degree_plus).astype(BF)
    grad_window = dot(table, grad_scaled, ((1,), (0,)))
    from_next = lax.ppermute(
        grad_window[:BAND].astype(BF), "blk", [((i + 1) % blk, i) for i in range(blk)]
    ).astype(F32)
    from_prev = lax.ppermute(
        grad_window[BAND + nodes :].astype(BF), "blk", [(i, (i + 1) % blk) for i in range(blk)]
    ).astype(F32)
    own = grad_window[BAND : BAND + nodes]
    grad_in = jnp.concatenate(
        [own[:BAND] + from_prev, own[BAND : nodes - BAND], own[nodes - BAND :] + from_next]
    )
    return grad_in, grad_weight, grad_bias


def local(features, neighbours, degree, weight_one, bias_one, weight_two, bias_two, cotangent):
    table = count_table(neighbours[0], degree[0])
    degree_plus = degree[0].astype(F32)[:, None] + 1.0
    averaged_one, preact_one = aggregate(features[0], table, degree_plus, weight_one, bias_one)
    hidden = jax.nn.gelu(preact_one).astype(BF)
    averaged_two, preact_two = aggregate(hidden, table, degree_plus, weight_two, bias_two)
    activations = jax.nn.gelu(preact_two).astype(BF)
    grad_hidden, grad_w_two, grad_b_two = layer_back(
        cotangent[0].astype(F32), preact_two, averaged_two, table, degree_plus, weight_two
    )
    grad_input, grad_w_one, grad_b_one = layer_back(
        grad_hidden, preact_one, averaged_one, table, degree_plus, weight_one
    )
    return (
        activations[None],
        grad_input.astype(BF)[None],
        grad_w_one,
        grad_b_one,
        grad_w_two,
        grad_b_two,
    )


def solution(mesh):
    rows = P("grp", "blk", None)
    spread = ("blk", "grp")
    return jax.shard_map(
        local,
        mesh=mesh,
        in_specs=(rows, rows, P("grp", "blk"), P(), P(), P(), P(), rows),
        out_specs=(rows, rows, P(spread, None), P(spread), P(spread, None), P(spread)),
        check_vma=False,
    )
```

```python
import jax
import jax.numpy as jnp
from jax import lax
from jax.experimental import pallas as pl
from jax.experimental.pallas import tpu as pltpu
from jax.sharding import PartitionSpec as P

BAND = 256
BF = jnp.bfloat16
F32 = jnp.float32
LANES = 128
STEP = 512
PARTS = 2
VMEM = 56 << 20
SCALE = 0.7978845608
CUBIC = 0.044715


def dot(a, b, contract=((1,), (0,))):
    return lax.dot_general(a, b, (contract, ((), ())), preferred_element_type=F32)


def sds(shape, dtype):
    return jax.ShapeDtypeStruct(shape, dtype)


def call(body, steps, in_specs, out_specs, out_shape, flops, scratch=(), prefetch=0, after=()):
    inputs = prefetch + len(in_specs)
    in_specs = list(in_specs) + [pl.BlockSpec(memory_space=pl.ANY)] * len(after)

    def kernel(*refs):
        body(*refs[:inputs], *refs[inputs + len(after) :])

    made = pl.pallas_call(
        kernel,
        grid_spec=pltpu.PrefetchScalarGridSpec(
            num_scalar_prefetch=prefetch,
            grid=(steps,),
            in_specs=in_specs,
            out_specs=out_specs,
            scratch_shapes=scratch,
        ),
        out_shape=out_shape,
        compiler_params=pltpu.CompilerParams(vmem_limit_bytes=VMEM),
        cost_estimate=pl.CostEstimate(flops=flops, bytes_accessed=1 << 12, transcendentals=0),
    )
    return lambda *args: made(*args, *after)


def full(shape):
    return pl.BlockSpec(shape, lambda j, *_: (0,) * len(shape))


def cols(rows, base=0, count=None, width=STEP, start=0):
    if count is None:
        return pl.BlockSpec((rows, width), lambda j, *_: (0, start + j))
    return pl.BlockSpec((rows, width), lambda j, *_: (0, jnp.clip(j - base, 0, count - 1)))


def rows_of(width, base, count, height=STEP):
    return pl.BlockSpec((height, width), lambda j, *_: (jnp.clip(j - base, 0, count - 1), 0))


def count_own(core, slots, degree, field):
    nodes, slot_total = slots.shape
    width = field.shape[1]
    quarter = (nodes + 2 * BAND) // 4
    groups, steps = nodes // LANES, width // STEP
    pieces = LANES // 8

    def count(core_ref, slots_ref, degree_ref, t_own, t_halo, n_own, n_halo, key_ref, value_ref):
        group = pl.program_id(0)
        slot = slots_ref[...]
        q = (
            (slot >= quarter).astype(jnp.int32)
            + (slot >= 2 * quarter).astype(jnp.int32)
            + (slot >= 3 * quarter).astype(jnp.int32)
        )
        used = lax.broadcasted_iota(jnp.int32, slot.shape, 0) < degree_ref[...]
        key_ref[...] = slot - q * quarter
        value_ref[...] = jnp.where(used, jnp.left_shift(1, q * 8), 0)
        sub = lax.broadcasted_iota(jnp.int32, (8, LANES), 0)
        row = lax.broadcasted_iota(jnp.int32, (LANES, LANES), 0)
        col = lax.broadcasted_iota(jnp.int32, (LANES, LANES), 1)
        nodes_at = pl.ds(pl.multiple_of(group * LANES, LANES), LANES)
        for part in range(quarter // LANES):

            def add_slot(k, packed):
                key = jnp.broadcast_to(key_ref[pl.ds(k, 1), :], (8, LANES)) - sub
                value = jnp.broadcast_to(value_ref[pl.ds(k, 1), :], (8, LANES))
                return tuple(
                    acc + jnp.where(key == part * LANES + 8 * i, value, 0)
                    for i, acc in enumerate(packed)
                )

            packed = lax.fori_loop(
                0,
                slot_total,
                add_slot,
                tuple(jnp.zeros((8, LANES), jnp.int32) for _ in range(pieces)),
                unroll=4,
            )
            packed = jnp.concatenate(packed, axis=0)
            for q in range(4):
                counts = jnp.bitwise_and(jnp.right_shift(packed, 8 * q), 255)
                start = q * quarter + part * LANES
                own = start - BAND
                if 0 <= own < nodes:
                    counts = counts + jnp.where(row + own == col + group * LANES, 2, 0)
                    counts = counts.astype(F32)
                    t_own[own : own + LANES, :] = counts.astype(BF)
                    n_own[nodes_at, own : own + LANES] = counts.T.astype(BF)
                else:
                    after = own >= 0
                    inner = start - nodes - BAND if after else start
                    slot_of = core_ref[0] if after else 1 - core_ref[0]
                    at = pl.ds(pl.multiple_of(slot_of * BAND + inner, LANES), LANES)
                    counts = counts.astype(F32)
                    t_halo[at, :] = counts.astype(BF)
                    n_halo[nodes_at, at] = counts.T.astype(BF)

    def body(core_ref, slots_ref, degree_ref, f_ref, t_own, t_halo, n_own, n_halo, out, *scratch):
        step = pl.program_id(0)

        @pl.when(step < groups)
        def _():
            count(core_ref, slots_ref, degree_ref, t_own, t_halo, n_own, n_halo, *scratch)

        @pl.when(step >= groups)
        def _():
            out[...] = dot(n_own[...], f_ref[...]).astype(BF)

    tall = lambda h: cols(h, 0, groups, LANES)
    return call(
        body,
        groups + steps,
        [tall(slot_total), tall(1), cols(nodes, groups, steps)],
        [
            tall(nodes),
            tall(2 * BAND),
            full((nodes, nodes)),
            full((nodes, 2 * BAND)),
            cols(nodes, groups, steps),
        ],
        [
            sds((nodes, nodes), BF),
            sds((2 * BAND, nodes), BF),
            sds((nodes, nodes), BF),
            sds((nodes, 2 * BAND), BF),
            sds((nodes, width), BF),
        ],
        flops=20 << 30,
        scratch=[pltpu.VMEM((slot_total, LANES), jnp.int32)] * 2,
        prefetch=1,
    )(core, slots.T, degree[None, :], field)


def own_sum(n_own, field):
    def body(n_ref, f_ref, out):
        out[...] = dot(n_ref[...], f_ref[...]).astype(BF)

    nodes, width = field.shape
    return call(
        body,
        width // STEP,
        [full((nodes, nodes)), cols(nodes)],
        cols(nodes),
        sds((nodes, width), BF),
        flops=2 * nodes * nodes * width,
    )(n_own, field)


def gelu_parts(p):
    square = p * p
    t = jnp.tanh(p * (SCALE + SCALE * CUBIC * square))
    half = 0.5 + 0.5 * t
    slope = half + (0.5 * p) * (1.0 - t * t) * (SCALE + 3.0 * SCALE * CUBIC * square)
    return p * half, slope


def average_step(own_ref, n_ref, near_ref, far_ref, inv_ref, out_t, averaged_ref, step):
    total = own_ref[...].astype(F32) + dot(n_ref[:, :BAND], near_ref[...])
    total = (total + dot(n_ref[:, BAND:], far_ref[...])) * inv_ref[...]
    averaged_ref[step] = total.astype(BF)
    out_t[...] = total.T.astype(BF)


def average_specs(nodes, steps):
    return [
        cols(nodes, 0, steps),
        full((nodes, 2 * BAND)),
        cols(BAND, 0, steps),
        cols(BAND, 0, steps),
        full((nodes, 1)),
    ]


def blocks_dot(blocks_ref, other, across=False):
    total = None
    for k in range(blocks_ref.shape[0]):
        if across:
            part = dot(blocks_ref[k], other[:, k * STEP : (k + 1) * STEP], ((1,), (1,)))
        else:
            part = dot(blocks_ref[k], other[k * STEP : (k + 1) * STEP, :])
        total = part if total is None else total + part
    return total


def first_layer(own, n_halo, near, far, inverse, weight, bias):
    nodes, width = own.shape
    steps = width // STEP

    def body(own_ref, n_ref, near_ref, far_ref, inv_ref, w_ref, b_ref, out_t, hidden, slope, avg):
        step = pl.program_id(0)

        @pl.when(step < steps)
        def _():
            average_step(own_ref, n_ref, near_ref, far_ref, inv_ref, out_t, avg, step)

        @pl.when(step >= steps)
        def _():
            value, grad = gelu_parts(blocks_dot(avg, w_ref) + b_ref[...])
            hidden[...] = value.astype(BF)
            slope[...] = grad.astype(BF)

    return call(
        body,
        2 * steps,
        average_specs(nodes, steps) + [cols(width, steps, steps), cols(1, steps, steps)],
        [rows_of(nodes, 0, steps), cols(nodes, steps, steps), cols(nodes, steps, steps)],
        [sds((width, nodes), BF), sds((nodes, width), BF), sds((nodes, width), BF)],
        flops=2 * nodes * width * (2 * BAND + width),
        scratch=[pltpu.VMEM((steps, nodes, STEP), BF)],
    )(own, n_halo, near, far, inverse, weight, bias)


def second_layer(own, n_halo, near, far, inverse, weight, bias, cotangent, t_halo):
    nodes, width = own.shape
    steps = width // STEP

    def body(
        own_ref, n_ref, near_ref, far_ref, inv_ref, w_ref, b_ref, c_ref, wt_ref, t_ref,
        out_t, activations, grad_pre, scaled, ends, avg, grads,
    ):
        step = pl.program_id(0)

        @pl.when(step < steps)
        def _():
            average_step(own_ref, n_ref, near_ref, far_ref, inv_ref, out_t, avg, step)

        @pl.when((step >= steps) & (step < 2 * steps))
        def _():
            value, grad = gelu_parts(blocks_dot(avg, w_ref) + b_ref[...])
            activations[...] = value.astype(BF)
            grad = (c_ref[...].astype(F32) * grad).astype(BF)
            grad_pre[...] = grad
            grads[step - steps] = grad

        @pl.when(step >= 2 * steps)
        def _():
            back_step(blocks_dot(grads, wt_ref, True), inv_ref, t_ref, scaled, ends)

    return call(
        body,
        3 * steps,
        average_specs(nodes, steps)
        + [
            cols(width, steps, steps),
            cols(1, steps, steps),
            cols(nodes, steps, steps),
            rows_of(width, 2 * steps, steps),
            full((2 * BAND, nodes)),
        ],
        [
            rows_of(nodes, 0, steps),
            cols(nodes, steps, steps),
            cols(nodes, steps, steps),
            cols(nodes, 2 * steps, steps),
            cols(2 * BAND, 2 * steps, steps),
        ],
        [
            sds((width, nodes), BF),
            sds((nodes, width), BF),
            sds((nodes, width), BF),
            sds((nodes, width), BF),
            sds((2 * BAND, width), BF),
        ],
        flops=2 * nodes * width * (4 * BAND + 2 * width),
        scratch=[pltpu.VMEM((steps, nodes, STEP), BF)] * 2,
    )(own, n_halo, near, far, inverse, weight, bias, cotangent, weight, t_halo)


def back_step(grad_averaged, inv_ref, t_ref, scaled_ref, ends_ref):
    scaled = (grad_averaged * inv_ref[...]).astype(BF)
    scaled_ref[...] = scaled
    ends_ref[...] = dot(t_ref[...], scaled).astype(BF)


def back_product(grad_pre, weight, inverse, t_halo, after=()):
    nodes, width = grad_pre[0].shape[0], weight.shape[1]
    steps = width // STEP

    def body(*refs):
        g_refs, (w_ref, inv_ref, t_ref, scaled, ends, token) = refs[:PARTS], refs[PARTS:]
        token[0] = 0
        total, at = 0.0, 0
        for g_ref in g_refs:
            size = g_ref.shape[1]
            total = total + dot(g_ref[...], w_ref[:, at : at + size], ((1,), (1,)))
            at += size
        back_step(total, inv_ref, t_ref, scaled, ends)

    return call(
        body,
        steps,
        [full(g.shape) for g in grad_pre]
        + [
            rows_of(width, 0, steps),
            full((nodes, 1)),
            full((2 * BAND, nodes)),
        ],
        [cols(nodes), cols(2 * BAND), pl.BlockSpec(memory_space=pltpu.SMEM)],
        [sds((nodes, width), BF), sds((2 * BAND, width), BF), sds((1,), jnp.int32)],
        flops=2 * nodes * width * (width + 2 * BAND),
        after=after,
    )(*grad_pre, weight, inverse, t_halo)


def back_sum_step(core_ref, s_ref, t_ref, near_ref, far_ref, slope_ref):
    nodes = t_ref.shape[0]
    total = dot(t_ref[...], s_ref[...])
    near, far = near_ref[...].astype(F32), far_ref[...].astype(F32)
    odd = core_ref[0] == 1
    pieces = (
        (0, BAND, total[:BAND] + jnp.where(odd, near, far)),
        (BAND, nodes - BAND, total[BAND : nodes - BAND]),
        (nodes - BAND, nodes, total[nodes - BAND :] + jnp.where(odd, far, near)),
    )
    for lo, hi, value in pieces:
        if slope_ref is not None:
            value = value * slope_ref[lo:hi, :].astype(F32)
        yield lo, hi, value.astype(BF)


def back_sum(core, scaled, t_own, near, far, after=()):
    def body(core_ref, s_ref, t_ref, near_ref, far_ref, out, token):
        token[0] = 0
        for lo, hi, value in back_sum_step(core_ref, s_ref, t_ref, near_ref, far_ref, None):
            out[lo:hi, :] = value

    nodes, width = scaled.shape
    return call(
        body,
        width // STEP,
        [cols(nodes), full((nodes, nodes)), cols(BAND), cols(BAND)],
        [cols(nodes), pl.BlockSpec(memory_space=pltpu.SMEM)],
        [sds((nodes, width), BF), sds((1,), jnp.int32)],
        flops=2 * nodes * nodes * width,
        prefetch=1,
        after=after,
    )(core, scaled, t_own, near, far)


def half_view(averaged_t):
    width, nodes = averaged_t.shape
    blk = lax.axis_size("blk")
    return averaged_t.reshape(blk // 2, 2, width // blk, nodes)


def half_spec(view, flip):
    pairs, _, run, nodes = view.shape
    pick = lambda j, core: (0, 1 - core[0] if flip else core[0], 0, 0)
    return pl.BlockSpec((pairs, 1, run, nodes), pick)


def half_dot(a_ref, g):
    pairs, _, run, nodes = a_ref.shape
    return dot(a_ref[...].reshape(pairs * run, nodes), g).astype(BF)


def weight_half(core, averaged_t, grad_pre, flip, after=()):
    width = sum(g.shape[1] for g in grad_pre)
    nodes = grad_pre[0].shape[0]
    view = half_view(averaged_t)
    half = view.shape[0] * view.shape[2]
    each = width // PARTS // STEP

    def part_cols(rows, part):
        return cols(rows, part * each, each)

    def body(core_ref, a_ref, *refs):
        g_refs, outs, bias = refs[: len(grad_pre)], refs[len(grad_pre) :][:PARTS], refs[-1]
        for part in range(PARTS):

            @pl.when(pl.program_id(0) // each == part)
            def _():
                g_ref = g_refs[part % len(g_refs)]
                outs[part][...] = half_dot(a_ref, g_ref[...])
                if flip:
                    bias[...] = jnp.sum(g_ref[...].astype(F32), axis=0, keepdims=True)

    if len(grad_pre) == 1:
        g_specs = [cols(nodes)]
    else:
        g_specs = [part_cols(nodes, part) for part in range(PARTS)]
    return call(
        body,
        width // STEP,
        [half_spec(view, flip)] + g_specs,
        [part_cols(half, part) for part in range(PARTS)] + [cols(1)] * flip,
        [sds((half, width // PARTS), BF)] * PARTS + [sds((1, width), F32)] * flip,
        flops=(2 if flip else 16) * nodes * half * width,
        prefetch=1,
        after=after,
    )(core, view, *grad_pre)


def back_sum_weight(core, scaled, t_own, near, far, slope, averaged_t, part, after=()):
    nodes, width = scaled.shape
    view = half_view(averaged_t)
    half = view.shape[0] * view.shape[2]
    width //= PARTS
    start = part * width // STEP

    def body(core_ref, s_ref, t_ref, near_ref, far_ref, p_ref, a_ref, grad_pre, send, bias):
        for lo, hi, value in back_sum_step(core_ref, s_ref, t_ref, near_ref, far_ref, p_ref):
            grad_pre[lo:hi, :] = value
        grad = grad_pre[...]
        bias[...] = jnp.sum(grad.astype(F32), axis=0, keepdims=True)
        send[...] = half_dot(a_ref, grad)

    return call(
        body,
        width // STEP,
        [
            cols(nodes, start=start),
            full((nodes, nodes)),
            cols(BAND, start=start),
            cols(BAND, start=start),
            cols(nodes, start=start),
            half_spec(view, True),
        ],
        [cols(nodes), cols(half), cols(1)],
        [sds((nodes, width), BF), sds((half, width), BF), sds((1, width), F32)],
        flops=2 * nodes * width * (nodes + half),
        prefetch=1,
        after=after,
    )(core, scaled, t_own, near, far, slope, view)


def swap(axis, distance):
    return [(i, i ^ distance) for i in range(lax.axis_size(axis))]


def exchange(near, far):
    count = lax.axis_size("blk")
    other = [(i, (i + 1 if i % 2 else i - 1) % count) for i in range(count)]
    return lax.ppermute(near, "blk", swap("blk", 1)), lax.ppermute(far, "blk", other)


def field_halo(field):
    nodes = field.shape[0]
    odd = lax.axis_index("blk") % 2
    rows = lambda last: lax.dynamic_slice_in_dim(field, last * (nodes - BAND), BAND, 0)
    return exchange(rows(1 - odd), rows(odd))


def place_bits():
    b, g = lax.axis_index("blk"), lax.axis_index("grp")
    line = (lax.axis_size("blk") // 4).bit_length() - 1
    across = lax.axis_size("grp").bit_length() - 1
    bits = [(b // (4 << i)) % 2 for i in reversed(range(line))] + [(b // 2) % 2]
    return bits + [(g // (1 << i)) % 2 for i in reversed(range(across))]


def steps_of(axis):
    line = (lax.axis_size("blk") // 4).bit_length() - 1
    across = lax.axis_size("grp").bit_length() - 1
    if axis == "y":
        return [(line, "blk", 2)]
    if axis == "x":
        return [(line + 1 + i, "grp", 1 << (across - 1 - i)) for i in range(across)]
    return [(line - 1 - axis, "blk", 4 << axis)] if axis < line else []


class PartSum:
    def __init__(self, terms, order):
        self.bits = place_bits()
        self.terms = [t.reshape((2,) * len(self.bits) + (-1, t.shape[-1])) for t in terms]
        self.todo = [step for axis in order for step in steps_of(axis)]
        self.settled = []

    def sum(self, flip=None, token=0):
        total = 0.0
        for term in self.terms:
            at, sizes = [], []
            for dim, bit in enumerate(self.bits):
                pick = term.shape[dim] == 2 and dim in self.settled
                at.append((1 - bit if dim == flip else bit) + token if pick else 0)
                sizes.append(1 if pick else term.shape[dim])
            total = total + lax.dynamic_slice(
                term, (*at, 0, 0), (*sizes, *term.shape[-2:])
            ).astype(F32)
        return total

    def step(self, token=0):
        dim, axis, distance = self.todo.pop(0)
        self.settled.append(dim)
        sent = self.sum(dim, token).astype(self.terms[0].dtype)
        self.terms = self.terms + [lax.ppermute(sent, axis, swap(axis, distance))]
        return sent

    def result(self):
        while self.todo:
            self.step()
        return self.sum().reshape(self.terms[0].shape[-2:])


def orders(kind):
    rest = range(1, (lax.axis_size("blk") // 4).bit_length() - 1)
    return {
        "xyz": ["x", "y", 0, *rest],
        "yxz": ["y", "x", 0, *rest],
        "xzy": ["x", 0, *rest, "y"],
        "zxy": [0, "x", *rest, "y"],
        "xzyz": ["x", 0, "y", *rest],
        "zxyz": [0, "x", "y", *rest],
    }[kind]


class WeightSum:
    def __init__(self, send, keep, kinds):
        self.parts = [
            PartSum([mine, lax.ppermute(theirs, "blk", swap("blk", 1))], orders(kind))
            for mine, theirs, kind in zip(keep, send, kinds)
        ]

    def step(self, token=0):
        return [part.step(token) for part in self.parts]

    def result(self):
        return jnp.concatenate([part.result() for part in self.parts], axis=1)


def bias_sum(biases, token):
    blk, grp = lax.axis_size("blk"), lax.axis_size("grp")
    bit = lax.axis_index("blk") % 2
    count = biases.shape[0]
    by_core = biases.reshape(count, blk // 2, 2, grp, -1).transpose(2, 1, 3, 0, 4)
    half = lambda which: lax.dynamic_index_in_dim(by_core, which + token, 0, keepdims=False)
    total = half(bit) + lax.ppermute(half(1 - bit), "blk", swap("blk", 1))
    return PartSum([total.reshape(blk // 2 * grp * count, -1)], orders("xyz")).result()


def local(features, neighbours, degree, weight_one, bias_one, weight_two, bias_two, cotangent):
    core = (lax.axis_index("blk") % 2).reshape(1).astype(jnp.int32)
    inverse = 1.0 / (degree[0].astype(F32)[:, None] + 1.0)
    field = features[0]

    near, far = field_halo(field)
    t_own, t_halo, n_own, n_halo, own = count_own(core, neighbours[0], degree[0], field)
    averaged_one, hidden, slope = first_layer(
        own, n_halo, near, far, inverse, weight_one, bias_one[None, :]
    )
    near, far = field_halo(hidden)
    own = own_sum(n_own, hidden)
    averaged_two, activations, grad_pre_two, scaled, ends = second_layer(
        own, n_halo, near, far, inverse, weight_two, bias_two[None, :], cotangent[0], t_halo
    )
    near, far = exchange(ends[:BAND], ends[BAND:])
    *send, grad_bias_two = weight_half(core, averaged_two, [grad_pre_two], True)
    keep = weight_half(core, averaged_two, [grad_pre_two], False, send)
    sum_two = WeightSum(send, keep, ["xyz", "yxz"])

    grad_pre_one, sends, grad_bias_one, after = [], [], [], sum_two.step()
    for part in range(PARTS):
        grad, send, bias = back_sum_weight(
            core, scaled, t_own, near, far, slope, averaged_one, part, after
        )
        grad_pre_one.append(grad)
        sends.append(send)
        grad_bias_one.append(bias)
        after = [send]
    keep = weight_half(core, averaged_one, grad_pre_one, False, sends)
    sum_one = WeightSum(sends, keep, ["xzyz", "zxyz"])
    sent = sum_one.step()
    scaled, ends, token = back_product(grad_pre_one, weight_one, inverse, t_halo, sent)
    near, far = exchange(ends[:BAND], ends[BAND:])
    sent = sum_two.step(token[0]) + sum_one.step(token[0])
    grad_input, token = back_sum(core, scaled, t_own, near, far, sent)
    sum_one.step(token[0])
    sum_two.step(token[0])
    grad_one, grad_two = sum_one.result(), sum_two.result()
    grad_bias_one = jnp.concatenate(grad_bias_one, axis=1)
    biases = bias_sum(jnp.concatenate([grad_bias_one, grad_bias_two]), token[0])
    return activations[None], grad_input[None], grad_one, biases[0], grad_two, biases[1]


def solution(mesh):
    rows = P("grp", "blk", None)
    spread = ("blk", "grp")
    return jax.shard_map(
        local,
        mesh=mesh,
        in_specs=(rows, rows, P("grp", "blk"), P(), P(), P(), P(), rows),
        out_specs=(rows, rows, P(spread, None), P(spread), P(spread, None), P(spread)),
        check_vma=False,
    )
```

```python
import math

import jax
import jax.numpy as jnp
from jax import lax
from jax.experimental import pallas as pl
from jax.experimental.pallas import tpu as pltpu
from jax.sharding import PartitionSpec as P

BAND = 256
BF = jnp.bfloat16
F32 = jnp.float32
LANES = 128
STEP = 512
PARTS = 2
ROOM = 6 << 20
VALUES = 16 << 20
ALPHA, W1, W2, WB = 1.0, 8, 8, 2
SCALE = 0.7978845608
CUBIC = 0.044715


def dot(a, b, contract=((1,), (0,))):
    return lax.dot_general(a, b, (contract, ((), ())), preferred_element_type=F32)


def sds(shape, dtype):
    return jax.ShapeDtypeStruct(shape, dtype)


def call(body, steps, in_specs, out_specs, out_shape, flops, scratch=(), prefetch=0, after=()):
    inputs = prefetch + len(in_specs)
    specs = list(in_specs) + [pl.BlockSpec(memory_space=pl.ANY)] * len(after)

    def kernel(*refs):
        body(*refs[:inputs], *refs[inputs + len(after) :])

    def run(*args):
        several = isinstance(out_shape, list)
        outs = zip(out_specs, out_shape) if several else [(out_specs, out_shape)]
        need = ROOM
        for spec, array in [*zip(in_specs, args[prefetch:]), *outs]:
            if spec.block_shape is not None:
                copies = 1 if spec.pipeline_mode is not None else 2
                need += copies * math.prod(spec.block_shape) * array.dtype.itemsize
        need += sum(math.prod(ref.shape) * jnp.dtype(ref.dtype).itemsize for ref in scratch)
        return pl.pallas_call(
            kernel,
            grid_spec=pltpu.PrefetchScalarGridSpec(
                num_scalar_prefetch=prefetch,
                grid=(steps,),
                in_specs=specs,
                out_specs=out_specs,
                scratch_shapes=scratch,
            ),
            out_shape=out_shape,
            compiler_params=pltpu.CompilerParams(vmem_limit_bytes=need),
            cost_estimate=pl.CostEstimate(flops=flops, bytes_accessed=1 << 12, transcendentals=0),
        )(*args, *after)

    return run


def full(shape):
    pick = lambda j, *_: (0,) * len(shape)
    return pl.BlockSpec(shape, pick, pipeline_mode=pl.Buffered(1))


def cols(rows, base=0, count=None, width=STEP, start=0):
    if count is None:
        return pl.BlockSpec((rows, width), lambda j, *_: (0, start + j))
    return pl.BlockSpec((rows, width), lambda j, *_: (0, jnp.clip(j - base, 0, count - 1)))


WHOLE = pl.BlockSpec(memory_space=pltpu.VMEM)
SCALAR = pl.BlockSpec(memory_space=pltpu.SMEM)
ANY = pl.BlockSpec(memory_space=pl.ANY)


def whole_call(body, in_specs, out_specs, out_shape, flops, scratch=(), after=()):
    inputs = len(in_specs)

    def kernel(*refs):
        body(*refs[:inputs], *refs[inputs + len(after) :])

    held = sum(
        math.prod(ref.shape) * jnp.dtype(ref.dtype).itemsize
        for ref in scratch
        if ref.memory_space == pltpu.VMEM
    )
    made = pl.pallas_call(
        kernel,
        in_specs=list(in_specs) + [ANY] * len(after),
        out_specs=out_specs,
        out_shape=out_shape,
        scratch_shapes=scratch,
        compiler_params=pltpu.CompilerParams(vmem_limit_bytes=VALUES + held),
        cost_estimate=pl.CostEstimate(flops=int(flops * ALPHA), bytes_accessed=1 << 12, transcendentals=0),
    )
    return lambda *args: made(*args, *after)


def blocks(width, step=STEP):
    return [slice(at, at + step) for at in range(0, width, step)]


def count_own(core, slots, degree, field):
    nodes, slot_total = slots.shape
    width = field.shape[1]
    quarter = (nodes + 2 * BAND) // 4
    groups, steps = nodes // LANES, width // STEP
    pieces = LANES // 8

    def count(core_ref, slots_ref, degree_ref, t_own, t_halo, n_own, n_halo, key_ref, value_ref):
        group = pl.program_id(0)
        slot = slots_ref[...]
        q = (
            (slot >= quarter).astype(jnp.int32)
            + (slot >= 2 * quarter).astype(jnp.int32)
            + (slot >= 3 * quarter).astype(jnp.int32)
        )
        used = lax.broadcasted_iota(jnp.int32, slot.shape, 0) < degree_ref[...]
        key_ref[...] = slot - q * quarter
        value_ref[...] = jnp.where(used, jnp.left_shift(1, q * 8), 0)
        sub = lax.broadcasted_iota(jnp.int32, (8, LANES), 0)
        row = lax.broadcasted_iota(jnp.int32, (LANES, LANES), 0)
        col = lax.broadcasted_iota(jnp.int32, (LANES, LANES), 1)
        nodes_at = pl.ds(pl.multiple_of(group * LANES, LANES), LANES)
        for part in range(quarter // LANES):

            def add_slot(k, packed):
                key = jnp.broadcast_to(key_ref[pl.ds(k, 1), :], (8, LANES)) - sub
                value = jnp.broadcast_to(value_ref[pl.ds(k, 1), :], (8, LANES))
                return tuple(
                    acc + jnp.where(key == part * LANES + 8 * i, value, 0)
                    for i, acc in enumerate(packed)
                )

            packed = lax.fori_loop(
                0,
                slot_total,
                add_slot,
                tuple(jnp.zeros((8, LANES), jnp.int32) for _ in range(pieces)),
                unroll=4,
            )
            packed = jnp.concatenate(packed, axis=0)
            for q in range(4):
                counts = jnp.bitwise_and(jnp.right_shift(packed, 8 * q), 255)
                start = q * quarter + part * LANES
                own = start - BAND
                if 0 <= own < nodes:
                    counts = counts + jnp.where(row + own == col + group * LANES, 2, 0)
                    counts = counts.astype(F32)
                    t_own[own : own + LANES, :] = counts.astype(BF)
                    n_own[nodes_at, own : own + LANES] = counts.T.astype(BF)
                else:
                    after = own >= 0
                    inner = start - nodes - BAND if after else start
                    slot_of = core_ref[0] if after else 1 - core_ref[0]
                    at = pl.ds(pl.multiple_of(slot_of * BAND + inner, LANES), LANES)
                    counts = counts.astype(F32)
                    t_halo[at, :] = counts.astype(BF)
                    n_halo[nodes_at, at] = counts.T.astype(BF)

    def body(core_ref, slots_ref, degree_ref, f_ref, t_own, t_halo, n_own, n_halo, out, *scratch):
        step = pl.program_id(0)

        @pl.when(step < groups)
        def _():
            count(core_ref, slots_ref, degree_ref, t_own, t_halo, n_own, n_halo, *scratch)

        @pl.when(step >= groups)
        def _():
            out[...] = dot(n_own[...], f_ref[...]).astype(BF)

    tall = lambda h: cols(h, 0, groups, LANES)
    return call(
        body,
        groups + steps,
        [tall(slot_total), tall(1), cols(nodes, groups, steps)],
        [
            tall(nodes),
            tall(2 * BAND),
            full((nodes, nodes)),
            full((nodes, 2 * BAND)),
            cols(nodes, groups, steps),
        ],
        [
            sds((nodes, nodes), BF),
            sds((2 * BAND, nodes), BF),
            sds((nodes, nodes), BF),
            sds((nodes, 2 * BAND), BF),
            sds((nodes, width), BF),
        ],
        flops=20 << 30,
        scratch=[pltpu.VMEM((slot_total, LANES), jnp.int32)] * 2,
        prefetch=1,
    )(core, slots.T, degree[None, :], field)


def own_sum(n_own, field):
    def body(n_ref, f_ref, out):
        for at in blocks(width):
            out[:, at] = dot(n_ref[...], f_ref[:, at]).astype(BF)

    nodes, width = field.shape
    return whole_call(
        body,
        [WHOLE] * 2,
        WHOLE,
        sds((nodes, width), BF),
        flops=2 * nodes * nodes * width,
    )(n_own, field)


def gelu_parts(p):
    square = p * p
    half = 0.5 + 0.5 * jnp.tanh(p * (SCALE + SCALE * CUBIC * square))
    value = p * half
    return value, half + (value - value * half) * (2.0 * SCALE + 6.0 * SCALE * CUBIC * square)


def layer(own, n_halo, near, far, inverse, weight, bias, cotangent=None):
    last = cotangent is not None
    nodes, width = own.shape

    def body(own_ref, n_ref, near_ref, far_ref, inv_ref, w_ref, b_ref, *refs):
        c_ref = refs[0] if last else None
        out_t, out, out_grad, avg, *rest = refs[1:] if last else refs
        for at in blocks(width):
            total = own_ref[:, at].astype(F32) + dot(n_ref[:, :BAND], near_ref[:, at])
            total = (total + dot(n_ref[:, BAND:], far_ref[:, at])) * inv_ref[...]
            avg[:, at] = total.astype(BF)
            out_t[at, :] = total.T.astype(BF)
        copies = []
        for i, at in enumerate(blocks(width)):
            value, grad = gelu_parts(dot(avg[...], w_ref[:, at]) + b_ref[:, at])
            if last:
                made, sems = rest
                made[:, at] = value.astype(BF)
                copies.append(pltpu.make_async_copy(made.at[:, at], out.at[:, at], sems.at[i]))
                copies[-1].start()
                grad = c_ref[:, at].astype(F32) * grad
            else:
                out[:, at] = value.astype(BF)
            out_grad[:, at] = grad.astype(BF)
        for copy in copies:
            copy.wait()

    scratch = [pltpu.VMEM((nodes, width), BF)]
    if last:
        scratch += [pltpu.VMEM((nodes, width), BF), pltpu.SemaphoreType.DMA((width // STEP,))]
    return whole_call(
        body,
        [WHOLE] * (7 + last),
        [WHOLE, ANY if last else WHOLE, WHOLE],
        [sds((width, nodes), BF), sds((nodes, width), BF), sds((nodes, width), BF)],
        flops=2 * nodes * width * (2 * BAND + width),
        scratch=scratch,
    )(own, n_halo, near, far, inverse, weight, bias, *([cotangent] if last else []))


def back_product(grad_pre, weight, inverse, t_halo, after=()):
    nodes, width = grad_pre[0].shape[0], weight.shape[1]
    count = len(grad_pre)

    def body(*refs):
        g_refs, (w_ref, inv_ref, t_ref, scaled, ends, token) = refs[:count], refs[count:]
        token[0] = 0
        for at in blocks(width):
            total, k = None, 0
            for g_ref in g_refs:
                size = g_ref.shape[1]
                part = dot(g_ref[...], w_ref[at, k : k + size], ((1,), (1,)))
                total = part if total is None else total + part
                k += size
            value = (total * inv_ref[...]).astype(BF)
            scaled[:, at] = value
            ends[:, at] = dot(t_ref[...], value).astype(BF)

    return whole_call(
        body,
        [WHOLE] * (count + 3),
        [WHOLE, WHOLE, SCALAR],
        [sds((nodes, width), BF), sds((2 * BAND, width), BF), sds((1,), jnp.int32)],
        flops=2 * nodes * width * (width + 2 * BAND),
        after=after,
    )(*grad_pre, weight, inverse, t_halo)


def back_sum_step(core_ref, s_ref, t_ref, near_ref, far_ref, slope_ref, at):
    nodes = t_ref.shape[0]
    total = dot(t_ref[...], s_ref[:, at])
    near, far = near_ref[:, at].astype(F32), far_ref[:, at].astype(F32)
    odd = core_ref[0] == 1
    pieces = (
        (0, BAND, total[:BAND] + jnp.where(odd, near, far)),
        (BAND, nodes - BAND, total[BAND : nodes - BAND]),
        (nodes - BAND, nodes, total[nodes - BAND :] + jnp.where(odd, far, near)),
    )
    for lo, hi, value in pieces:
        if slope_ref is not None:
            value = value * slope_ref[lo:hi, at].astype(F32)
        yield lo, hi, value.astype(BF)


def back_sum(core, scaled, t_own, near, far, after=()):
    nodes, width = scaled.shape

    def body(core_ref, s_ref, t_ref, near_ref, far_ref, out, token, made, sems):
        token[0] = 0
        copies = []
        for i, at in enumerate(blocks(width)):
            for lo, hi, value in back_sum_step(
                core_ref, s_ref, t_ref, near_ref, far_ref, None, at
            ):
                made[lo:hi, at] = value
            copies.append(pltpu.make_async_copy(made.at[:, at], out.at[:, at], sems.at[i]))
            copies[-1].start()
        for copy in copies:
            copy.wait()

    return whole_call(
        body,
        [SCALAR] + [WHOLE] * 4,
        [ANY, SCALAR],
        [sds((nodes, width), BF), sds((1,), jnp.int32)],
        flops=WB * nodes * nodes * width,
        scratch=[pltpu.VMEM((nodes, width), BF), pltpu.SemaphoreType.DMA((width // STEP,))],
        after=after,
    )(core, scaled, t_own, near, far)


def half_rows(a_ref, which):
    picked = a_ref[:, which]
    return picked.reshape(picked.shape[0] * picked.shape[1], picked.shape[2])


def by_core(rows):
    blk = lax.axis_size("blk")
    return rows.reshape(blk // 2, 2, rows.shape[0] // blk, rows.shape[1])


def weight_half(core, averaged_t, grad_pre, flip, extra=None, after=(), weigh=1):
    view = by_core(averaged_t)
    nodes = grad_pre[0].shape[0]
    half = averaged_t.shape[0] // 2
    count = len(grad_pre)
    more = [] if extra is None else [by_core(extra)]

    def body(core_ref, a_ref, *refs):
        g_refs, refs = refs[:count], refs[count:]
        e_refs, outs, bias = refs[: len(more)], refs[len(more) :][:count], refs[len(more) + count :]
        which = 1 - core_ref[0] if flip else core_ref[0]
        rows = half_rows(a_ref, which)
        for i, (g_ref, out) in enumerate(zip(g_refs, outs)):
            for at in blocks(g_ref.shape[1]):
                out[:, at] = dot(rows, g_ref[:, at]).astype(BF)
            if flip:
                bias[i][...] = jnp.sum(g_ref[...].astype(F32), axis=0, keepdims=True)
        for e_ref in e_refs:
            outs[-1][:, g_refs[-1].shape[1] :] = half_rows(e_ref, which)

    widths = [g.shape[1] for g in grad_pre]
    shapes = [sds((half, w), BF) for w in widths]
    if more:
        shapes[-1] = sds((half, widths[-1] + extra.shape[1]), BF)
    return whole_call(
        body,
        [SCALAR] + [WHOLE] * (1 + count + len(more)),
        [WHOLE] * (count * (1 + flip)),
        shapes + [sds((1, w), F32) for w in widths] * flip,
        flops=2 * nodes * half * sum(widths) * weigh,
        after=after,
    )(core, view, *grad_pre, *more)


def back_sum_weight(core, scaled, t_own, near, far, slope, averaged_t, part, biases=None, after=()):
    nodes, width = scaled.shape
    whole = width
    width //= PARTS
    view = by_core(averaged_t)
    half = averaged_t.shape[0] // 2
    start = part * width
    given = [] if biases is None else list(biases)

    def body(core_ref, s_ref, t_ref, near_ref, far_ref, p_ref, a_ref, *refs):
        given_refs, (grad_pre, send, bias, *rest) = refs[: len(given)], refs[len(given) :]
        rows = half_rows(a_ref, 1 - core_ref[0])
        for out_at, at in zip(blocks(width), blocks(whole)[start // STEP :]):
            for lo, hi, value in back_sum_step(
                core_ref, s_ref, t_ref, near_ref, far_ref, p_ref, at
            ):
                grad_pre[lo:hi, out_at] = value
            grad = grad_pre[:, out_at]
            bias[:, out_at] = jnp.sum(grad.astype(F32), axis=0, keepdims=True)
            send[:, out_at] = dot(rows, grad).astype(BF)
        if given:
            one, two = [*given_refs[:part], bias], given_refs[part:]
            lane = lax.broadcasted_iota(jnp.int32, (LANES, LANES), 1)
            spread = rest[1]
            for at in blocks(whole, LANES):
                columns = []
                for refs in (one, two):
                    size = refs[0].shape[1]
                    ref, k = refs[at.start // size], at.start % size
                    columns.append(jnp.broadcast_to(ref[:, k : k + LANES], (LANES, LANES)).T)
                mixed = jnp.where(lane < LANES // 2, *columns).astype(BF)
                rest[0][at, :] = mixed
                spread[at, :] = mixed
            run = view.shape[2]
            picked = spread.reshape(whole // (2 * run), 2, run, LANES)
            send[:, width:] = half_rows(picked, 1 - core_ref[0])

    columns = width + (LANES if given else 0)
    shapes = [sds((nodes, width), BF), sds((half, columns), BF), sds((1, width), F32)]
    return whole_call(
        body,
        [SCALAR] + [WHOLE] * (6 + len(given)),
        [WHOLE] * (3 + bool(given)),
        shapes + [sds((whole, LANES), BF)] * bool(given),
        flops=2 * nodes * width * (nodes + half),
        scratch=[pltpu.VMEM((whole, LANES), BF)] * bool(given),
        after=after,
    )(core, scaled, t_own, near, far, slope, view, *given)


def swap(axis, distance):
    return [(i, i ^ distance) for i in range(lax.axis_size(axis))]


def exchange(near, far):
    count = lax.axis_size("blk")
    other = [(i, (i + 1 if i % 2 else i - 1) % count) for i in range(count)]
    return lax.ppermute(near, "blk", swap("blk", 1)), lax.ppermute(far, "blk", other)


def field_halo(field):
    nodes = field.shape[0]
    odd = lax.axis_index("blk") % 2
    rows = lambda last: lax.dynamic_slice_in_dim(field, last * (nodes - BAND), BAND, 0)
    return exchange(rows(1 - odd), rows(odd))


def place_bits():
    b, g = lax.axis_index("blk"), lax.axis_index("grp")
    line = (lax.axis_size("blk") // 4).bit_length() - 1
    across = lax.axis_size("grp").bit_length() - 1
    bits = [(b // (4 << i)) % 2 for i in reversed(range(line))] + [(b // 2) % 2]
    return bits + [(g // (1 << i)) % 2 for i in reversed(range(across))]


def steps_of(axis):
    line = (lax.axis_size("blk") // 4).bit_length() - 1
    across = lax.axis_size("grp").bit_length() - 1
    if axis == "y":
        return [(line, "blk", 2)]
    if axis == "x":
        return [(line + 1 + i, "grp", 1 << (across - 1 - i)) for i in range(across)]
    return [(line - 1 - axis, "blk", 4 << axis)] if axis < line else []


class PartSum:
    def __init__(self, send, keep, order):
        self.bits = place_bits()
        terms = [keep, lax.ppermute(send, "blk", swap("blk", 1))]
        self.terms = [t.reshape((2,) * len(self.bits) + (-1, t.shape[-1])) for t in terms]
        self.todo = [step for axis in orders(order) for step in steps_of(axis)]
        self.settled = []

    def sum(self, flip=None, token=0):
        total = 0.0
        for term in self.terms:
            at, sizes = [], []
            for dim, bit in enumerate(self.bits):
                pick = term.shape[dim] == 2 and dim in self.settled
                at.append((1 - bit if dim == flip else bit) + token if pick else 0)
                sizes.append(1 if pick else term.shape[dim])
            total = total + lax.dynamic_slice(
                term, (*at, 0, 0), (*sizes, *term.shape[-2:])
            ).astype(F32)
        return total

    def step(self, token=0):
        dim, axis, distance = self.todo.pop(0)
        self.settled.append(dim)
        sent = self.sum(dim, token).astype(BF)
        self.terms = self.terms + [lax.ppermute(sent, axis, swap(axis, distance))]
        return sent

    def result(self):
        while self.todo:
            self.step()
        return self.sum().reshape(self.terms[0].shape[-2:])


def joint_step(parts, token=0):
    dim, axis, distance = parts[0].todo[0]
    sent = []
    for part in parts:
        part.todo.pop(0)
        part.settled.append(dim)
        sent.append(part.sum(dim, token).astype(BF))
    sent = jnp.concatenate(sent, axis=-1)
    received = lax.ppermute(sent, axis, swap(axis, distance))
    at = 0
    for part in parts:
        width = part.terms[0].shape[-1]
        part.terms = part.terms + [received[..., at : at + width]]
        at += width
    return sent


def advance(parts, token=0):
    if not parts[0].todo:
        return []
    if len(parts) > 1 and all(part.todo == parts[0].todo for part in parts):
        return [joint_step(parts, token)]
    return [part.step(token) for part in parts]


def orders(kind):
    rest = range(1, (lax.axis_size("blk") // 4).bit_length() - 1)
    return {
        "xyz": ["x", "y", 0, *rest],
        "yxz": ["y", "x", 0, *rest],
        "zxyz": [0, "x", "y", *rest],
        "xzyz": ["x", 0, "y", *rest],
        "yzxz": ["y", 0, "x", *rest],
        "zyxz": [0, "y", "x", *rest],
    }[kind]


def local(features, neighbours, degree, weight_one, bias_one, weight_two, bias_two, cotangent):
    core = (lax.axis_index("blk") % 2).reshape(1).astype(jnp.int32)
    inverse = 1.0 / (degree[0].astype(F32)[:, None] + 1.0)
    field = features[0]
    width = field.shape[1]

    near, far = field_halo(field)
    t_own, t_halo, n_own, n_halo, own = count_own(core, neighbours[0], degree[0], field)
    averaged_one, hidden, slope = layer(
        own, n_halo, near, far, inverse, weight_one, bias_one[None, :]
    )
    near, far = field_halo(hidden)
    own = own_sum(n_own, hidden)
    averaged_two, activations, grad_pre_two = layer(
        own, n_halo, near, far, inverse, weight_two, bias_two[None, :], cotangent[0]
    )
    scaled, ends, _ = back_product([grad_pre_two], weight_two, inverse, t_halo)
    near, far = exchange(ends[:BAND], ends[BAND:])

    send, bias_two = weight_half(core, averaged_two, [grad_pre_two], True)
    (keep,) = weight_half(core, averaged_two, [grad_pre_two], False, None, [send], W2)
    two = [PartSum(send, keep, "zxyz")]
    sent = advance(two)

    grad_a, send_a, grad_bias_a = back_sum_weight(
        core, scaled, t_own, near, far, slope, averaged_one, 0, None, sent
    )
    grad_b, send_b, _, extra = back_sum_weight(
        core, scaled, t_own, near, far, slope, averaged_one, 1, [grad_bias_a, bias_two]
    )
    keep = weight_half(core, averaged_one, [grad_a, grad_b], False, extra, [], W1)
    orders_one = ("xzyz", "yxz")
    one = [PartSum(s, k, order) for s, k, order in zip((send_a, send_b), keep, orders_one)]
    sent = advance(one)
    scaled, ends, token = back_product([grad_a, grad_b], weight_one, inverse, t_halo, sent)
    near, far = exchange(ends[:BAND], ends[BAND:])

    sent = advance(two, token[0]) + advance(one, token[0])
    sent = advance(two) + advance(one)
    grad_input, token = back_sum(core, scaled, t_own, near, far, sent)
    while one[0].todo:
        advance(two, token[0])
        advance(one, token[0])
    grad_two = jnp.concatenate([part.result() for part in two], axis=1)
    parts = [part.result() for part in one]
    grad_one = jnp.concatenate([parts[0], parts[1][:, : width // 2]], axis=1)
    biases = [parts[1][:, width // 2 + LANES // 2 * i] for i in range(2)]
    return activations[None], grad_input[None], grad_one, biases[0], grad_two, biases[1]


def solution(mesh):
    rows = P("grp", "blk", None)
    spread = ("blk", "grp")
    return jax.shard_map(
        local,
        mesh=mesh,
        in_specs=(rows, rows, P("grp", "blk"), P(), P(), P(), P(), rows),
        out_specs=(rows, rows, P(spread, None), P(spread), P(spread, None), P(spread)),
        check_vma=False,
    )
```

```python
import math

import jax
import jax.numpy as jnp
from jax import lax
from jax.experimental import pallas as pl
from jax.experimental.pallas import tpu as pltpu
from jax.sharding import PartitionSpec as P

BAND = 256
BF = jnp.bfloat16
F32 = jnp.float32
LANES = 128
STEP = 512
PARTS = 2
ROOM = 6 << 20
VALUES = 12 << 20
SCALE = 0.7978845608
CUBIC = 0.044715


def dot(a, b, contract=((1,), (0,))):
    return lax.dot_general(a, b, (contract, ((), ())), preferred_element_type=F32)


def sds(shape, dtype):
    return jax.ShapeDtypeStruct(shape, dtype)


def call(body, steps, in_specs, out_specs, out_shape, flops, scratch=(), prefetch=0, after=()):
    inputs = prefetch + len(in_specs)
    specs = list(in_specs) + [pl.BlockSpec(memory_space=pl.ANY)] * len(after)

    def kernel(*refs):
        body(*refs[:inputs], *refs[inputs + len(after) :])

    def run(*args):
        several = isinstance(out_shape, list)
        outs = zip(out_specs, out_shape) if several else [(out_specs, out_shape)]
        need = ROOM
        for spec, array in [*zip(in_specs, args[prefetch:]), *outs]:
            if spec.block_shape is not None:
                copies = 1 if spec.pipeline_mode is not None else 2
                need += copies * math.prod(spec.block_shape) * array.dtype.itemsize
        need += sum(math.prod(ref.shape) * jnp.dtype(ref.dtype).itemsize for ref in scratch)
        return pl.pallas_call(
            kernel,
            grid_spec=pltpu.PrefetchScalarGridSpec(
                num_scalar_prefetch=prefetch,
                grid=(steps,),
                in_specs=specs,
                out_specs=out_specs,
                scratch_shapes=scratch,
            ),
            out_shape=out_shape,
            compiler_params=pltpu.CompilerParams(vmem_limit_bytes=need),
            cost_estimate=pl.CostEstimate(flops=flops, bytes_accessed=1 << 12, transcendentals=0),
        )(*args, *after)

    return run


def full(shape):
    pick = lambda j, *_: (0,) * len(shape)
    return pl.BlockSpec(shape, pick, pipeline_mode=pl.Buffered(1))


def cols(rows, base=0, count=None, width=STEP, start=0):
    if count is None:
        return pl.BlockSpec((rows, width), lambda j, *_: (0, start + j))
    return pl.BlockSpec((rows, width), lambda j, *_: (0, jnp.clip(j - base, 0, count - 1)))


WHOLE = pl.BlockSpec(memory_space=pltpu.VMEM)
SCALAR = pl.BlockSpec(memory_space=pltpu.SMEM)
ANY = pl.BlockSpec(memory_space=pl.ANY)


def whole_call(body, in_specs, out_specs, out_shape, flops, scratch=(), after=()):
    inputs = len(in_specs)

    def kernel(*refs):
        body(*refs[:inputs], *refs[inputs + len(after) :])

    held = sum(
        math.prod(ref.shape) * jnp.dtype(ref.dtype).itemsize
        for ref in scratch
        if ref.memory_space == pltpu.VMEM
    )
    made = pl.pallas_call(
        kernel,
        in_specs=list(in_specs) + [ANY] * len(after),
        out_specs=out_specs,
        out_shape=out_shape,
        scratch_shapes=scratch,
        compiler_params=pltpu.CompilerParams(vmem_limit_bytes=VALUES + held),
        cost_estimate=pl.CostEstimate(flops=flops, bytes_accessed=1 << 12, transcendentals=0),
    )
    return lambda *args: made(*args, *after)


def blocks(width, step=STEP):
    return [slice(at, at + step) for at in range(0, width, step)]


def count_own(core, slots, degree, field):
    nodes, slot_total = slots.shape
    width = field.shape[1]
    quarter = (nodes + 2 * BAND) // 4
    groups, steps = nodes // LANES, width // STEP
    pieces = LANES // 8

    def count(core_ref, slots_ref, degree_ref, t_own, t_halo, n_own, n_halo, key_ref, value_ref):
        group = pl.program_id(0)
        slot = slots_ref[...]
        q = (
            (slot >= quarter).astype(jnp.int32)
            + (slot >= 2 * quarter).astype(jnp.int32)
            + (slot >= 3 * quarter).astype(jnp.int32)
        )
        used = lax.broadcasted_iota(jnp.int32, slot.shape, 0) < degree_ref[...]
        key_ref[...] = slot - q * quarter
        value_ref[...] = jnp.where(used, jnp.left_shift(1, q * 8), 0)
        sub = lax.broadcasted_iota(jnp.int32, (8, LANES), 0)
        row = lax.broadcasted_iota(jnp.int32, (LANES, LANES), 0)
        col = lax.broadcasted_iota(jnp.int32, (LANES, LANES), 1)
        nodes_at = pl.ds(pl.multiple_of(group * LANES, LANES), LANES)
        for part in range(quarter // LANES):

            def add_slot(k, packed):
                key = jnp.broadcast_to(key_ref[pl.ds(k, 1), :], (8, LANES)) - sub
                value = jnp.broadcast_to(value_ref[pl.ds(k, 1), :], (8, LANES))
                return tuple(
                    acc + jnp.where(key == part * LANES + 8 * i, value, 0)
                    for i, acc in enumerate(packed)
                )

            packed = lax.fori_loop(
                0,
                slot_total,
                add_slot,
                tuple(jnp.zeros((8, LANES), jnp.int32) for _ in range(pieces)),
                unroll=4,
            )
            packed = jnp.concatenate(packed, axis=0)
            for q in range(4):
                counts = jnp.bitwise_and(jnp.right_shift(packed, 8 * q), 255)
                start = q * quarter + part * LANES
                own = start - BAND
                if 0 <= own < nodes:
                    counts = counts + jnp.where(row + own == col + group * LANES, 2, 0)
                    counts = counts.astype(F32)
                    t_own[own : own + LANES, :] = counts.astype(BF)
                    n_own[nodes_at, own : own + LANES] = counts.T.astype(BF)
                else:
                    after = own >= 0
                    inner = start - nodes - BAND if after else start
                    slot_of = core_ref[0] if after else 1 - core_ref[0]
                    at = pl.ds(pl.multiple_of(slot_of * BAND + inner, LANES), LANES)
                    counts = counts.astype(F32)
                    t_halo[at, :] = counts.astype(BF)
                    n_halo[nodes_at, at] = counts.T.astype(BF)

    def body(core_ref, slots_ref, degree_ref, f_ref, t_own, t_halo, n_own, n_halo, out, *scratch):
        step = pl.program_id(0)

        @pl.when(step < groups)
        def _():
            count(core_ref, slots_ref, degree_ref, t_own, t_halo, n_own, n_halo, *scratch)

        @pl.when(step >= groups)
        def _():
            out[...] = dot(n_own[...], f_ref[...]).astype(BF)

    tall = lambda h: cols(h, 0, groups, LANES)
    return call(
        body,
        groups + steps,
        [tall(slot_total), tall(1), cols(nodes, groups, steps)],
        [
            tall(nodes),
            tall(2 * BAND),
            full((nodes, nodes)),
            full((nodes, 2 * BAND)),
            cols(nodes, groups, steps),
        ],
        [
            sds((nodes, nodes), BF),
            sds((2 * BAND, nodes), BF),
            sds((nodes, nodes), BF),
            sds((nodes, 2 * BAND), BF),
            sds((nodes, width), BF),
        ],
        flops=20 << 30,
        scratch=[pltpu.VMEM((slot_total, LANES), jnp.int32)] * 2,
        prefetch=1,
    )(core, slots.T, degree[None, :], field)


def own_sum(n_own, field):
    def body(n_ref, f_ref, out):
        for at in blocks(width):
            out[:, at] = dot(n_ref[...], f_ref[:, at]).astype(BF)

    nodes, width = field.shape
    return whole_call(
        body,
        [WHOLE] * 2,
        WHOLE,
        sds((nodes, width), BF),
        flops=2 * nodes * nodes * width,
    )(n_own, field)


def gelu_parts(p):
    square = p * p
    half = 0.5 + 0.5 * jnp.tanh(p * (SCALE + SCALE * CUBIC * square))
    value = p * half
    return value, half + (value - value * half) * (2.0 * SCALE + 6.0 * SCALE * CUBIC * square)


def layer(own, n_halo, near, far, inverse, weight, bias, cotangent=None):
    last = cotangent is not None
    nodes, width = own.shape
    grads = PARTS if last else 1

    def body(own_ref, n_ref, near_ref, far_ref, inv_ref, w_ref, b_ref, *refs):
        c_ref = refs[0] if last else None
        out_t, out, *refs = refs[1:] if last else refs
        out_grads, (avg, *rest) = refs[:grads], refs[grads:]
        for at in blocks(width):
            total = own_ref[:, at].astype(F32) + dot(n_ref[:, :BAND], near_ref[:, at])
            total = (total + dot(n_ref[:, BAND:], far_ref[:, at])) * inv_ref[...]
            avg[:, at] = total.astype(BF)
            out_t[at, :] = total.T.astype(BF)
        copies = []
        for i, at in enumerate(blocks(width)):
            value, grad = gelu_parts(dot(avg[...], w_ref[:, at]) + b_ref[:, at])
            if last:
                made, sems = rest
                made[:, at] = value.astype(BF)
                copies.append(pltpu.make_async_copy(made.at[:, at], out.at[:, at], sems.at[i]))
                copies[-1].start()
                grad = c_ref[:, at].astype(F32) * grad
            else:
                out[:, at] = value.astype(BF)
            part, k = divmod(at.start, width // grads)
            out_grads[part][:, k : k + STEP] = grad.astype(BF)
        for copy in copies:
            copy.wait()

    scratch = [pltpu.VMEM((nodes, width), BF)]
    if last:
        scratch += [pltpu.VMEM((nodes, width), BF), pltpu.SemaphoreType.DMA((width // STEP,))]
    return whole_call(
        body,
        [WHOLE] * (7 + last),
        [WHOLE, ANY if last else WHOLE] + [WHOLE] * grads,
        [sds((width, nodes), BF), sds((nodes, width), BF)]
        + [sds((nodes, width // grads), BF)] * grads,
        flops=2 * nodes * width * (2 * BAND + width),
        scratch=scratch,
    )(own, n_halo, near, far, inverse, weight, bias, *([cotangent] if last else []))


def back_product(grad_pre, weight, inverse, t_halo, after=()):
    nodes, width = grad_pre[0].shape[0], weight.shape[1]
    count = len(grad_pre)

    def body(*refs):
        g_refs, (w_ref, inv_ref, t_ref, scaled, ends, token) = refs[:count], refs[count:]
        token[0] = 0
        for at in blocks(width):
            total, k = None, 0
            for g_ref in g_refs:
                size = g_ref.shape[1]
                part = dot(g_ref[...], w_ref[at, k : k + size], ((1,), (1,)))
                total = part if total is None else total + part
                k += size
            value = (total * inv_ref[...]).astype(BF)
            scaled[:, at] = value
            ends[:, at] = dot(t_ref[...], value).astype(BF)

    return whole_call(
        body,
        [WHOLE] * (count + 3),
        [WHOLE, WHOLE, SCALAR],
        [sds((nodes, width), BF), sds((2 * BAND, width), BF), sds((1,), jnp.int32)],
        flops=2 * nodes * width * (width + 2 * BAND),
        after=after,
    )(*grad_pre, weight, inverse, t_halo)


def back_sum_step(core_ref, s_ref, t_ref, near_ref, far_ref, slope_ref, at):
    nodes = t_ref.shape[0]
    total = dot(t_ref[...], s_ref[:, at])
    near, far = near_ref[:, at].astype(F32), far_ref[:, at].astype(F32)
    odd = core_ref[0] == 1
    pieces = (
        (0, BAND, total[:BAND] + jnp.where(odd, near, far)),
        (BAND, nodes - BAND, total[BAND : nodes - BAND]),
        (nodes - BAND, nodes, total[nodes - BAND :] + jnp.where(odd, far, near)),
    )
    for lo, hi, value in pieces:
        if slope_ref is not None:
            value = value * slope_ref[lo:hi, at].astype(F32)
        yield lo, hi, value.astype(BF)


def back_sum(core, scaled, t_own, near, far, after=()):
    nodes, width = scaled.shape

    def body(core_ref, s_ref, t_ref, near_ref, far_ref, out, token, made, sems):
        token[0] = 0
        copies = []
        for i, at in enumerate(blocks(width)):
            for lo, hi, value in back_sum_step(
                core_ref, s_ref, t_ref, near_ref, far_ref, None, at
            ):
                made[lo:hi, at] = value
            copies.append(pltpu.make_async_copy(made.at[:, at], out.at[:, at], sems.at[i]))
            copies[-1].start()
        for copy in copies:
            copy.wait()

    return whole_call(
        body,
        [SCALAR] + [WHOLE] * 4,
        [ANY, SCALAR],
        [sds((nodes, width), BF), sds((1,), jnp.int32)],
        flops=0,
        scratch=[pltpu.VMEM((nodes, width), BF), pltpu.SemaphoreType.DMA((width // STEP,))],
        after=after,
    )(core, scaled, t_own, near, far)


def half_rows(a_ref, which):
    picked = a_ref[:, which]
    return picked.reshape(picked.shape[0] * picked.shape[1], picked.shape[2])


def by_core(rows):
    blk = lax.axis_size("blk")
    return rows.reshape(blk // 2, 2, rows.shape[0] // blk, rows.shape[1])


def weight_half(core, averaged_t, grad_pre, flip, extra=None, after=(), weigh=1):
    view = by_core(averaged_t)
    nodes = grad_pre[0].shape[0]
    half = averaged_t.shape[0] // 2
    count = len(grad_pre)
    more = [] if extra is None else [by_core(extra)]

    def body(core_ref, a_ref, *refs):
        g_refs, refs = refs[:count], refs[count:]
        e_refs, outs, bias = refs[: len(more)], refs[len(more) :][:count], refs[len(more) + count :]
        which = 1 - core_ref[0] if flip else core_ref[0]
        rows = half_rows(a_ref, which)
        for i, (g_ref, out) in enumerate(zip(g_refs, outs)):
            for at in blocks(g_ref.shape[1]):
                out[:, at] = dot(rows, g_ref[:, at]).astype(BF)
            if flip:
                bias[i][...] = jnp.sum(g_ref[...].astype(F32), axis=0, keepdims=True)
        for e_ref in e_refs:
            outs[-1][:, g_refs[-1].shape[1] :] = half_rows(e_ref, which)

    widths = [g.shape[1] for g in grad_pre]
    shapes = [sds((half, w), BF) for w in widths]
    if more:
        shapes[-1] = sds((half, widths[-1] + extra.shape[1]), BF)
    return whole_call(
        body,
        [SCALAR] + [WHOLE] * (1 + count + len(more)),
        [WHOLE] * (count * (1 + flip)),
        shapes + [sds((1, w), F32) for w in widths] * flip,
        flops=2 * nodes * half * sum(widths) * weigh,
        after=after,
    )(core, view, *grad_pre, *more)


def back_sum_weight(core, scaled, t_own, near, far, slope, averaged_t, part, biases=None, after=()):
    nodes, width = scaled.shape
    whole = width
    width //= PARTS
    view = by_core(averaged_t)
    half = averaged_t.shape[0] // 2
    start = part * width
    given = [] if biases is None else list(biases)

    def body(core_ref, s_ref, t_ref, near_ref, far_ref, p_ref, a_ref, *refs):
        given_refs, (grad_pre, send, bias, *rest) = refs[: len(given)], refs[len(given) :]
        rows = half_rows(a_ref, 1 - core_ref[0])
        for out_at, at in zip(blocks(width), blocks(whole)[start // STEP :]):
            for lo, hi, value in back_sum_step(
                core_ref, s_ref, t_ref, near_ref, far_ref, p_ref, at
            ):
                grad_pre[lo:hi, out_at] = value
            grad = grad_pre[:, out_at]
            bias[:, out_at] = jnp.sum(grad.astype(F32), axis=0, keepdims=True)
            send[:, out_at] = dot(rows, grad).astype(BF)
        if given:
            one, two = [*given_refs[:part], bias], given_refs[part:]
            lane = lax.broadcasted_iota(jnp.int32, (LANES, LANES), 1)
            spread = rest[1]
            for at in blocks(whole, LANES):
                columns = []
                for refs in (one, two):
                    size = refs[0].shape[1]
                    ref, k = refs[at.start // size], at.start % size
                    columns.append(jnp.broadcast_to(ref[:, k : k + LANES], (LANES, LANES)).T)
                mixed = jnp.where(lane < LANES // 2, *columns).astype(BF)
                rest[0][at, :] = mixed
                spread[at, :] = mixed
            run = view.shape[2]
            picked = spread.reshape(whole // (2 * run), 2, run, LANES)
            send[:, width:] = half_rows(picked, 1 - core_ref[0])

    columns = width + (LANES if given else 0)
    shapes = [sds((nodes, width), BF), sds((half, columns), BF), sds((1, width), F32)]
    return whole_call(
        body,
        [SCALAR] + [WHOLE] * (6 + len(given)),
        [WHOLE] * (3 + bool(given)),
        shapes + [sds((whole, LANES), BF)] * bool(given),
        flops=2 * nodes * width * (nodes + half),
        scratch=[pltpu.VMEM((whole, LANES), BF)] * bool(given),
        after=after,
    )(core, scaled, t_own, near, far, slope, view, *given)


def swap(axis, distance):
    return [(i, i ^ distance) for i in range(lax.axis_size(axis))]


def exchange(near, far):
    count = lax.axis_size("blk")
    other = [(i, (i + 1 if i % 2 else i - 1) % count) for i in range(count)]
    return lax.ppermute(near, "blk", swap("blk", 1)), lax.ppermute(far, "blk", other)


def field_halo(field):
    nodes = field.shape[0]
    odd = lax.axis_index("blk") % 2
    rows = lambda last: lax.dynamic_slice_in_dim(field, last * (nodes - BAND), BAND, 0)
    return exchange(rows(1 - odd), rows(odd))


def place_bits():
    b, g = lax.axis_index("blk"), lax.axis_index("grp")
    line = (lax.axis_size("blk") // 4).bit_length() - 1
    across = lax.axis_size("grp").bit_length() - 1
    bits = [(b // (4 << i)) % 2 for i in reversed(range(line))] + [(b // 2) % 2]
    return bits + [(g // (1 << i)) % 2 for i in reversed(range(across))]


def steps_of(axis):
    line = (lax.axis_size("blk") // 4).bit_length() - 1
    across = lax.axis_size("grp").bit_length() - 1
    if axis == "y":
        return [(line, "blk", 2)]
    if axis == "x":
        return [(line + 1 + i, "grp", 1 << (across - 1 - i)) for i in range(across)]
    return [(line - 1 - axis, "blk", 4 << axis)] if axis < line else []


class PartSum:
    def __init__(self, send, keep, order):
        self.bits = place_bits()
        terms = [keep, lax.ppermute(send, "blk", swap("blk", 1))]
        self.terms = [t.reshape((2,) * len(self.bits) + (-1, t.shape[-1])) for t in terms]
        self.todo = [step for axis in orders(order) for step in steps_of(axis)]
        self.settled = []

    def sum(self, flip=None, token=0):
        total = 0.0
        for term in self.terms:
            at, sizes = [], []
            for dim, bit in enumerate(self.bits):
                pick = term.shape[dim] == 2 and dim in self.settled
                at.append((1 - bit if dim == flip else bit) + token if pick else 0)
                sizes.append(1 if pick else term.shape[dim])
            total = total + lax.dynamic_slice(
                term, (*at, 0, 0), (*sizes, *term.shape[-2:])
            ).astype(F32)
        return total

    def step(self, token=0):
        dim, axis, distance = self.todo.pop(0)
        self.settled.append(dim)
        sent = self.sum(dim, token).astype(BF)
        self.terms = self.terms + [lax.ppermute(sent, axis, swap(axis, distance))]
        return sent

    def result(self):
        while self.todo:
            self.step()
        return self.sum().reshape(self.terms[0].shape[-2:])


def joint_step(parts, token=0):
    dim, axis, distance = parts[0].todo[0]
    sent = []
    for part in parts:
        part.todo.pop(0)
        part.settled.append(dim)
        sent.append(part.sum(dim, token).astype(BF))
    sent = jnp.concatenate(sent, axis=-1)
    received = lax.ppermute(sent, axis, swap(axis, distance))
    at = 0
    for part in parts:
        width = part.terms[0].shape[-1]
        part.terms = part.terms + [received[..., at : at + width]]
        at += width
    return sent


def advance(parts, token=0):
    if not parts[0].todo:
        return []
    if len(parts) > 1 and all(part.todo == parts[0].todo for part in parts):
        return [joint_step(parts, token)]
    return [part.step(token) for part in parts]


def orders(kind):
    rest = range(1, (lax.axis_size("blk") // 4).bit_length() - 1)
    return {
        "xyz": ["x", "y", 0, *rest],
        "yxz": ["y", "x", 0, *rest],
        "zxyz": [0, "x", "y", *rest],
        "xzyz": ["x", 0, "y", *rest],
        "yzxz": ["y", 0, "x", *rest],
        "zyxz": [0, "y", "x", *rest],
    }[kind]


def local(features, neighbours, degree, weight_one, bias_one, weight_two, bias_two, cotangent):
    core = (lax.axis_index("blk") % 2).reshape(1).astype(jnp.int32)
    inverse = 1.0 / (degree[0].astype(F32)[:, None] + 1.0)
    field = features[0]
    width = field.shape[1]

    near, far = field_halo(field)
    t_own, t_halo, n_own, n_halo, own = count_own(core, neighbours[0], degree[0], field)
    averaged_one, hidden, slope = layer(
        own, n_halo, near, far, inverse, weight_one, bias_one[None, :]
    )
    near, far = field_halo(hidden)
    own = own_sum(n_own, hidden)
    averaged_two, activations, *halves = layer(
        own, n_halo, near, far, inverse, weight_two, bias_two[None, :], cotangent[0]
    )
    scaled, ends, _ = back_product(halves, weight_two, inverse, t_halo)
    near, far = exchange(ends[:BAND], ends[BAND:])

    *send, bias_a, bias_b = weight_half(core, averaged_two, halves, True)
    keep = weight_half(core, averaged_two, halves, False, None, send, 8)
    two = [PartSum(a, b, kind) for a, b, kind in zip(send, keep, ("xzyz","zxyz"))]
    sent = advance(two)

    grad_a, send_a, grad_bias_a = back_sum_weight(
        core, scaled, t_own, near, far, slope, averaged_one, 0, None, sent
    )
    grad_b, send_b, _, extra = back_sum_weight(
        core, scaled, t_own, near, far, slope, averaged_one, 1, [grad_bias_a, bias_a, bias_b]
    )
    keep = weight_half(core, averaged_one, [grad_a, grad_b], False, extra, [], 8)
    orders_one = ("yxz", "zxyz")
    one = [PartSum(s, k, order) for s, k, order in zip((send_a, send_b), keep, orders_one)]
    sent = advance(one) + advance(two)
    scaled, ends, token = back_product([grad_a, grad_b], weight_one, inverse, t_halo, sent)
    near, far = exchange(ends[:BAND], ends[BAND:])

    sent = advance(one, token[0])
    advance(two, token[0])
    advance(one)
    sent = advance(one)
    grad_input, token = back_sum(core, scaled, t_own, near, far, sent)
    while one[0].todo:
        advance(two, token[0])
        advance(one, token[0])
    grad_two = jnp.concatenate([part.result() for part in two], axis=1)
    parts = [part.result() for part in one]
    grad_one = jnp.concatenate([parts[0], parts[1][:, : width // 2]], axis=1)
    biases = [parts[1][:, width // 2 + LANES // 2 * i] for i in range(2)]
    return activations[None], grad_input[None], grad_one, biases[0], grad_two, biases[1]


def solution(mesh):
    rows = P("grp", "blk", None)
    spread = ("blk", "grp")
    return jax.shard_map(
        local,
        mesh=mesh,
        in_specs=(rows, rows, P("grp", "blk"), P(), P(), P(), P(), rows),
        out_specs=(rows, rows, P(spread, None), P(spread), P(spread, None), P(spread)),
        check_vma=False,
    )
```

```python
import math

import jax
import jax.numpy as jnp
from jax import lax
from jax.experimental import pallas as pl
from jax.experimental.pallas import tpu as pltpu
from jax.sharding import PartitionSpec as P

BAND = 256
BF = jnp.bfloat16
F32 = jnp.float32
LANES = 128
STEP = 512
PARTS = 2
ROOM = 6 << 20
VALUES = 12 << 20
SCALE = 0.7978845608
CUBIC = 0.044715


def dot(a, b, contract=((1,), (0,))):
    return lax.dot_general(a, b, (contract, ((), ())), preferred_element_type=F32)


def sds(shape, dtype):
    return jax.ShapeDtypeStruct(shape, dtype)


def call(body, steps, in_specs, out_specs, out_shape, flops, scratch=(), prefetch=0, after=()):
    inputs = prefetch + len(in_specs)
    specs = list(in_specs) + [pl.BlockSpec(memory_space=pl.ANY)] * len(after)

    def kernel(*refs):
        body(*refs[:inputs], *refs[inputs + len(after) :])

    def run(*args):
        several = isinstance(out_shape, list)
        outs = zip(out_specs, out_shape) if several else [(out_specs, out_shape)]
        need = ROOM
        for spec, array in [*zip(in_specs, args[prefetch:]), *outs]:
            if spec.block_shape is not None:
                copies = 1 if spec.pipeline_mode is not None else 2
                need += copies * math.prod(spec.block_shape) * array.dtype.itemsize
        need += sum(math.prod(ref.shape) * jnp.dtype(ref.dtype).itemsize for ref in scratch)
        return pl.pallas_call(
            kernel,
            grid_spec=pltpu.PrefetchScalarGridSpec(
                num_scalar_prefetch=prefetch,
                grid=(steps,),
                in_specs=specs,
                out_specs=out_specs,
                scratch_shapes=scratch,
            ),
            out_shape=out_shape,
            compiler_params=pltpu.CompilerParams(vmem_limit_bytes=need),
            cost_estimate=pl.CostEstimate(flops=flops, bytes_accessed=1 << 12, transcendentals=0),
        )(*args, *after)

    return run


def full(shape):
    pick = lambda j, *_: (0,) * len(shape)
    return pl.BlockSpec(shape, pick, pipeline_mode=pl.Buffered(1))


def cols(rows, base=0, count=None, width=STEP, start=0):
    if count is None:
        return pl.BlockSpec((rows, width), lambda j, *_: (0, start + j))
    return pl.BlockSpec((rows, width), lambda j, *_: (0, jnp.clip(j - base, 0, count - 1)))


WHOLE = pl.BlockSpec(memory_space=pltpu.VMEM)
SCALAR = pl.BlockSpec(memory_space=pltpu.SMEM)
ANY = pl.BlockSpec(memory_space=pl.ANY)


def whole_call(body, in_specs, out_specs, out_shape, flops, scratch=(), after=()):
    inputs = len(in_specs)

    def kernel(*refs):
        body(*refs[:inputs], *refs[inputs + len(after) :])

    held = sum(
        math.prod(ref.shape) * jnp.dtype(ref.dtype).itemsize
        for ref in scratch
        if ref.memory_space == pltpu.VMEM
    )
    made = pl.pallas_call(
        kernel,
        in_specs=list(in_specs) + [ANY] * len(after),
        out_specs=out_specs,
        out_shape=out_shape,
        scratch_shapes=scratch,
        compiler_params=pltpu.CompilerParams(vmem_limit_bytes=VALUES + held),
        cost_estimate=pl.CostEstimate(flops=flops, bytes_accessed=1 << 12, transcendentals=0),
    )
    return lambda *args: made(*args, *after)


def blocks(width, step=STEP):
    return [slice(at, at + step) for at in range(0, width, step)]


def count_own(core, slots, degree, field):
    nodes, slot_total = slots.shape
    width = field.shape[1]
    quarter = (nodes + 2 * BAND) // 4
    groups, steps = nodes // LANES, width // STEP
    pieces = LANES // 8

    def count(core_ref, slots_ref, degree_ref, t_own, t_halo, n_own, n_halo, key_ref, value_ref):
        group = pl.program_id(0)
        slot = slots_ref[...]
        q = (
            (slot >= quarter).astype(jnp.int32)
            + (slot >= 2 * quarter).astype(jnp.int32)
            + (slot >= 3 * quarter).astype(jnp.int32)
        )
        used = lax.broadcasted_iota(jnp.int32, slot.shape, 0) < degree_ref[...]
        key_ref[...] = slot - q * quarter
        value_ref[...] = jnp.where(used, jnp.left_shift(1, q * 8), 0)
        sub = lax.broadcasted_iota(jnp.int32, (8, LANES), 0)
        row = lax.broadcasted_iota(jnp.int32, (LANES, LANES), 0)
        col = lax.broadcasted_iota(jnp.int32, (LANES, LANES), 1)
        nodes_at = pl.ds(pl.multiple_of(group * LANES, LANES), LANES)
        for part in range(quarter // LANES):

            def add_slot(k, packed):
                key = jnp.broadcast_to(key_ref[pl.ds(k, 1), :], (8, LANES)) - sub
                value = jnp.broadcast_to(value_ref[pl.ds(k, 1), :], (8, LANES))
                return tuple(
                    acc + jnp.where(key == part * LANES + 8 * i, value, 0)
                    for i, acc in enumerate(packed)
                )

            packed = lax.fori_loop(
                0,
                slot_total,
                add_slot,
                tuple(jnp.zeros((8, LANES), jnp.int32) for _ in range(pieces)),
                unroll=4,
            )
            packed = jnp.concatenate(packed, axis=0)
            for q in range(4):
                counts = jnp.bitwise_and(jnp.right_shift(packed, 8 * q), 255)
                start = q * quarter + part * LANES
                own = start - BAND
                if 0 <= own < nodes:
                    counts = counts + jnp.where(row + own == col + group * LANES, 2, 0)
                    counts = counts.astype(F32)
                    t_own[own : own + LANES, :] = counts.astype(BF)
                    n_own[nodes_at, own : own + LANES] = counts.T.astype(BF)
                else:
                    after = own >= 0
                    inner = start - nodes - BAND if after else start
                    slot_of = core_ref[0] if after else 1 - core_ref[0]
                    at = pl.ds(pl.multiple_of(slot_of * BAND + inner, LANES), LANES)
                    counts = counts.astype(F32)
                    t_halo[at, :] = counts.astype(BF)
                    n_halo[nodes_at, at] = counts.T.astype(BF)

    def body(core_ref, slots_ref, degree_ref, f_ref, t_own, t_halo, n_own, n_halo, out, *scratch):
        step = pl.program_id(0)

        @pl.when(step < groups)
        def _():
            count(core_ref, slots_ref, degree_ref, t_own, t_halo, n_own, n_halo, *scratch)

        @pl.when(step >= groups)
        def _():
            out[...] = dot(n_own[...], f_ref[...]).astype(BF)

    tall = lambda h: cols(h, 0, groups, LANES)
    return call(
        body,
        groups + steps,
        [tall(slot_total), tall(1), cols(nodes, groups, steps)],
        [
            tall(nodes),
            tall(2 * BAND),
            full((nodes, nodes)),
            full((nodes, 2 * BAND)),
            cols(nodes, groups, steps),
        ],
        [
            sds((nodes, nodes), BF),
            sds((2 * BAND, nodes), BF),
            sds((nodes, nodes), BF),
            sds((nodes, 2 * BAND), BF),
            sds((nodes, width), BF),
        ],
        flops=20 << 30,
        scratch=[pltpu.VMEM((slot_total, LANES), jnp.int32)] * 2,
        prefetch=1,
    )(core, slots.T, degree[None, :], field)


def own_sum(n_own, field):
    def body(n_ref, f_ref, out):
        for at in blocks(width):
            out[:, at] = dot(n_ref[...], f_ref[:, at]).astype(BF)

    nodes, width = field.shape
    return whole_call(
        body,
        [WHOLE] * 2,
        WHOLE,
        sds((nodes, width), BF),
        flops=2 * nodes * nodes * width,
    )(n_own, field)


def gelu_parts(p):
    square = p * p
    half = 0.5 + 0.5 * jnp.tanh(p * (SCALE + SCALE * CUBIC * square))
    value = p * half
    return value, half + (value - value * half) * (2.0 * SCALE + 6.0 * SCALE * CUBIC * square)


def layer(core, own, n_halo, near, far, inverse, weight, bias, cotangent=None):
    last = cotangent is not None
    nodes, width = own.shape
    grads = PARTS if last else 1

    def body(core_ref, own_ref, n_ref, near_ref, far_ref, inv_ref, w_ref, b_ref, *refs):
        c_ref = refs[0] if last else None
        out_t, out, *refs = refs[1:] if last else refs
        if not last:
            to_near, to_far, *refs = refs
        out_grads, (avg, *rest) = refs[:grads], refs[grads:]
        for at in blocks(width):
            total = own_ref[:, at].astype(F32) + dot(n_ref[:, :BAND], near_ref[:, at])
            total = (total + dot(n_ref[:, BAND:], far_ref[:, at])) * inv_ref[...]
            avg[:, at] = total.astype(BF)
            out_t[at, :] = total.T.astype(BF)
        copies = []
        for i, at in enumerate(blocks(width)):
            value, grad = gelu_parts(dot(avg[...], w_ref[:, at]) + b_ref[:, at])
            if last:
                made, sems = rest
                made[:, at] = value.astype(BF)
                copies.append(pltpu.make_async_copy(made.at[:, at], out.at[:, at], sems.at[i]))
                copies[-1].start()
                grad = c_ref[:, at].astype(F32) * grad
            else:
                out[:, at] = value.astype(BF)
            part, k = divmod(at.start, width // grads)
            out_grads[part][:, k : k + STEP] = grad.astype(BF)
        if not last:
            end = nodes - BAND
            for to, at in ((to_near, (1 - core_ref[0]) * end), (to_far, core_ref[0] * end)):
                to[...] = out[pl.ds(pl.multiple_of(at, BAND), BAND), :]
        for copy in copies:
            copy.wait()

    scratch = [pltpu.VMEM((nodes, width), BF)]
    if last:
        scratch += [pltpu.VMEM((nodes, width), BF), pltpu.SemaphoreType.DMA((width // STEP,))]
    return whole_call(
        body,
        [SCALAR] + [WHOLE] * (7 + last),
        [WHOLE, ANY if last else WHOLE] + [WHOLE] * (2 if last else 3),
        [sds((width, nodes), BF), sds((nodes, width), BF)]
        + ([] if last else [sds((BAND, width), BF)] * 2)
        + [sds((nodes, width // grads), BF)] * grads,
        flops=2 * nodes * width * (2 * BAND + width),
        scratch=scratch,
    )(core, own, n_halo, near, far, inverse, weight, bias, *([cotangent] if last else []))


def back_product(grad_pre, weight, inverse, t_halo, after=()):
    nodes, width = grad_pre[0].shape[0], weight.shape[1]
    count = len(grad_pre)

    def body(*refs):
        g_refs, (w_ref, inv_ref, t_ref, scaled, ends, token) = refs[:count], refs[count:]
        token[0] = 0
        for at in blocks(width):
            total, k = None, 0
            for g_ref in g_refs:
                size = g_ref.shape[1]
                part = dot(g_ref[...], w_ref[at, k : k + size], ((1,), (1,)))
                total = part if total is None else total + part
                k += size
            value = (total * inv_ref[...]).astype(BF)
            scaled[:, at] = value
            ends[:, at] = dot(t_ref[...], value).astype(BF)

    return whole_call(
        body,
        [WHOLE] * (count + 3),
        [WHOLE, WHOLE, SCALAR],
        [sds((nodes, width), BF), sds((2 * BAND, width), BF), sds((1,), jnp.int32)],
        flops=2 * nodes * width * (width + 2 * BAND),
        after=after,
    )(*grad_pre, weight, inverse, t_halo)


def back_sum_step(core_ref, s_ref, t_ref, near_ref, far_ref, slope_ref, at):
    nodes = t_ref.shape[0]
    total = dot(t_ref[...], s_ref[:, at])
    near, far = near_ref[:, at].astype(F32), far_ref[:, at].astype(F32)
    odd = core_ref[0] == 1
    pieces = (
        (0, BAND, total[:BAND] + jnp.where(odd, near, far)),
        (BAND, nodes - BAND, total[BAND : nodes - BAND]),
        (nodes - BAND, nodes, total[nodes - BAND :] + jnp.where(odd, far, near)),
    )
    for lo, hi, value in pieces:
        if slope_ref is not None:
            value = value * slope_ref[lo:hi, at].astype(F32)
        yield lo, hi, value.astype(BF)


def back_sum(core, scaled, t_own, near, far, after=()):
    nodes, width = scaled.shape

    def body(core_ref, s_ref, t_ref, near_ref, far_ref, out, token, made, sems):
        token[0] = 0
        copies = []
        for i, at in enumerate(blocks(width)):
            for lo, hi, value in back_sum_step(
                core_ref, s_ref, t_ref, near_ref, far_ref, None, at
            ):
                made[lo:hi, at] = value
            copies.append(pltpu.make_async_copy(made.at[:, at], out.at[:, at], sems.at[i]))
            copies[-1].start()
        for copy in copies:
            copy.wait()

    return whole_call(
        body,
        [SCALAR] + [WHOLE] * 4,
        [ANY, SCALAR],
        [sds((nodes, width), BF), sds((1,), jnp.int32)],
        flops=0,
        scratch=[pltpu.VMEM((nodes, width), BF), pltpu.SemaphoreType.DMA((width // STEP,))],
        after=after,
    )(core, scaled, t_own, near, far)


def half_rows(a_ref, which):
    picked = a_ref[:, which]
    return picked.reshape(picked.shape[0] * picked.shape[1], picked.shape[2])


def by_core(rows):
    blk = lax.axis_size("blk")
    return rows.reshape(blk // 2, 2, rows.shape[0] // blk, rows.shape[1])


def weight_half(core, averaged_t, grad_pre, flip, extra=None, after=(), weigh=1):
    view = by_core(averaged_t)
    nodes = grad_pre[0].shape[0]
    half = averaged_t.shape[0] // 2
    count = len(grad_pre)
    more = [] if extra is None else [by_core(extra)]

    def body(core_ref, a_ref, *refs):
        g_refs, refs = refs[:count], refs[count:]
        e_refs, outs, bias = refs[: len(more)], refs[len(more) :][:count], refs[len(more) + count :]
        which = 1 - core_ref[0] if flip else core_ref[0]
        rows = half_rows(a_ref, which)
        for i, (g_ref, out) in enumerate(zip(g_refs, outs)):
            for at in blocks(g_ref.shape[1]):
                out[:, at] = dot(rows, g_ref[:, at]).astype(BF)
            if flip:
                bias[i][...] = jnp.sum(g_ref[...].astype(F32), axis=0, keepdims=True)
        for e_ref in e_refs:
            outs[-1][:, g_refs[-1].shape[1] :] = half_rows(e_ref, which)

    widths = [g.shape[1] for g in grad_pre]
    shapes = [sds((half, w), BF) for w in widths]
    if more:
        shapes[-1] = sds((half, widths[-1] + extra.shape[1]), BF)
    return whole_call(
        body,
        [SCALAR] + [WHOLE] * (1 + count + len(more)),
        [WHOLE] * (count * (1 + flip)),
        shapes + [sds((1, w), F32) for w in widths] * flip,
        flops=2 * nodes * half * sum(widths) * weigh,
        after=after,
    )(core, view, *grad_pre, *more)


def back_sum_weight(core, scaled, t_own, near, far, slope, averaged_t, part, biases=None, after=()):
    nodes, width = scaled.shape
    whole = width
    width //= PARTS
    view = by_core(averaged_t)
    half = averaged_t.shape[0] // 2
    start = part * width
    given = [] if biases is None else list(biases)

    def body(core_ref, s_ref, t_ref, near_ref, far_ref, p_ref, a_ref, *refs):
        given_refs, (grad_pre, send, bias, *rest) = refs[: len(given)], refs[len(given) :]
        rows = half_rows(a_ref, 1 - core_ref[0])
        for out_at, at in zip(blocks(width), blocks(whole)[start // STEP :]):
            for lo, hi, value in back_sum_step(
                core_ref, s_ref, t_ref, near_ref, far_ref, p_ref, at
            ):
                grad_pre[lo:hi, out_at] = value
            grad = grad_pre[:, out_at]
            bias[:, out_at] = jnp.sum(grad.astype(F32), axis=0, keepdims=True)
            send[:, out_at] = dot(rows, grad).astype(BF)
        if given:
            one, two = [*given_refs[:part], bias], given_refs[part:]
            lane = lax.broadcasted_iota(jnp.int32, (LANES, LANES), 1)
            spread = rest[1]
            for at in blocks(whole, LANES):
                columns = []
                for refs in (one, two):
                    size = refs[0].shape[1]
                    ref, k = refs[at.start // size], at.start % size
                    columns.append(jnp.broadcast_to(ref[:, k : k + LANES], (LANES, LANES)).T)
                mixed = jnp.where(lane < LANES // 2, *columns).astype(BF)
                rest[0][at, :] = mixed
                spread[at, :] = mixed
            run = view.shape[2]
            picked = spread.reshape(whole // (2 * run), 2, run, LANES)
            send[:, width:] = half_rows(picked, 1 - core_ref[0])

    columns = width + (LANES if given else 0)
    shapes = [sds((nodes, width), BF), sds((half, columns), BF), sds((1, width), F32)]
    return whole_call(
        body,
        [SCALAR] + [WHOLE] * (6 + len(given)),
        [WHOLE] * (3 + bool(given)),
        shapes + [sds((whole, LANES), BF)] * bool(given),
        flops=2 * nodes * width * (nodes + half),
        scratch=[pltpu.VMEM((whole, LANES), BF)] * bool(given),
        after=after,
    )(core, scaled, t_own, near, far, slope, view, *given)


def swap(axis, distance):
    return [(i, i ^ distance) for i in range(lax.axis_size(axis))]


def exchange(near, far):
    count = lax.axis_size("blk")
    other = [(i, (i + 1 if i % 2 else i - 1) % count) for i in range(count)]
    return lax.ppermute(near, "blk", swap("blk", 1)), lax.ppermute(far, "blk", other)


def field_halo(field):
    nodes = field.shape[0]
    odd = lax.axis_index("blk") % 2
    rows = lambda last: lax.dynamic_slice_in_dim(field, last * (nodes - BAND), BAND, 0)
    return exchange(rows(1 - odd), rows(odd))


def place_bits():
    b, g = lax.axis_index("blk"), lax.axis_index("grp")
    line = (lax.axis_size("blk") // 4).bit_length() - 1
    across = lax.axis_size("grp").bit_length() - 1
    bits = [(b // (4 << i)) % 2 for i in reversed(range(line))] + [(b // 2) % 2]
    return bits + [(g // (1 << i)) % 2 for i in reversed(range(across))]


def steps_of(axis):
    line = (lax.axis_size("blk") // 4).bit_length() - 1
    across = lax.axis_size("grp").bit_length() - 1
    if axis == "y":
        return [(line, "blk", 2)]
    if axis == "x":
        return [(line + 1 + i, "grp", 1 << (across - 1 - i)) for i in range(across)]
    return [(line - 1 - axis, "blk", 4 << axis)] if axis < line else []


class PartSum:
    def __init__(self, send, keep, order):
        self.bits = place_bits()
        terms = [keep, lax.ppermute(send, "blk", swap("blk", 1))]
        self.terms = [t.reshape((2,) * len(self.bits) + (-1, t.shape[-1])) for t in terms]
        self.todo = [step for axis in orders(order) for step in steps_of(axis)]
        self.settled = []

    def sum(self, flip=None, token=0):
        total = 0.0
        for term in self.terms:
            at, sizes = [], []
            for dim, bit in enumerate(self.bits):
                pick = term.shape[dim] == 2 and dim in self.settled
                at.append((1 - bit if dim == flip else bit) + token if pick else 0)
                sizes.append(1 if pick else term.shape[dim])
            total = total + lax.dynamic_slice(
                term, (*at, 0, 0), (*sizes, *term.shape[-2:])
            ).astype(F32)
        return total

    def step(self, token=0):
        dim, axis, distance = self.todo.pop(0)
        self.settled.append(dim)
        sent = self.sum(dim, token).astype(BF)
        self.terms = self.terms + [lax.ppermute(sent, axis, swap(axis, distance))]
        return sent

    def before_last(self):
        *self.terms, _ = self.terms
        return self.sum().reshape(self.terms[0].shape[-2:])

    def result(self):
        while self.todo:
            self.step()
        return self.sum().reshape(self.terms[0].shape[-2:])


def joint_step(parts, token=0):
    dim, axis, distance = parts[0].todo[0]
    sent = []
    for part in parts:
        part.todo.pop(0)
        part.settled.append(dim)
        sent.append(part.sum(dim, token).astype(BF))
    sent = jnp.concatenate(sent, axis=-1)
    received = lax.ppermute(sent, axis, swap(axis, distance))
    at = 0
    for part in parts:
        width = part.terms[0].shape[-1]
        part.terms = part.terms + [received[..., at : at + width]]
        at += width
        part.last = received
    return sent


def advance(parts, token=0):
    if not parts[0].todo:
        return []
    if len(parts) > 1 and all(part.todo == parts[0].todo for part in parts):
        return [joint_step(parts, token)]
    return [part.step(token) for part in parts]


def finish(parts):
    received = parts[0].last.reshape(-1, parts[0].last.shape[-1])
    sums = [part.before_last() for part in parts]
    rows = received.shape[0]
    width = received.shape[1] - LANES

    def body(*refs):
        *sum_refs, last_ref, out, bias_one, bias_two = refs
        at = 0
        for ref in sum_refs:
            to = min(at + ref.shape[1], width)
            out[:, at:to] = ref[:, : to - at] + last_ref[:, at:to].astype(F32)
            at = to
        tile = (sum_refs[-1][:, -LANES:] + last_ref[:, width:].astype(F32)).T
        bias_one[...] = tile[:1]
        bias_two[...] = tile[LANES // 2 : LANES // 2 + 1]

    out, bias_one, bias_two = whole_call(
        body,
        [WHOLE] * (1 + len(sums)),
        [WHOLE] * 3,
        [sds((rows, width), F32), sds((1, rows), F32), sds((1, rows), F32)],
        flops=0,
    )(*sums, received)
    return out, [bias_one[0], bias_two[0]]


def orders(kind):
    rest = range(1, (lax.axis_size("blk") // 4).bit_length() - 1)
    return {
        "xyz": ["x", "y", 0, *rest],
        "yxz": ["y", "x", 0, *rest],
        "zxyz": [0, "x", "y", *rest],
        "xzyz": ["x", 0, "y", *rest],
        "yzxz": ["y", 0, "x", *rest],
        "zyxz": [0, "y", "x", *rest],
    }[kind]


def local(features, neighbours, degree, weight_one, bias_one, weight_two, bias_two, cotangent):
    core = (lax.axis_index("blk") % 2).reshape(1).astype(jnp.int32)
    inverse = 1.0 / (degree[0].astype(F32)[:, None] + 1.0)
    field = features[0]
    width = field.shape[1]

    near, far = field_halo(field)
    t_own, t_halo, n_own, n_halo, own = count_own(core, neighbours[0], degree[0], field)
    averaged_one, hidden, near, far, slope = layer(
        core, own, n_halo, near, far, inverse, weight_one, bias_one[None, :]
    )
    near, far = exchange(near, far)
    own = own_sum(n_own, hidden)
    averaged_two, activations, *halves = layer(
        core, own, n_halo, near, far, inverse, weight_two, bias_two[None, :], cotangent[0]
    )
    scaled, ends, _ = back_product(halves, weight_two, inverse, t_halo)
    near, far = exchange(ends[:BAND], ends[BAND:])

    *send, bias_a, bias_b = weight_half(core, averaged_two, halves, True)
    keep = weight_half(core, averaged_two, halves, False, None, send, 8)
    two = [PartSum(a, b, kind) for a, b, kind in zip(send, keep, ("xzyz","zxyz"))]
    sent = advance(two)

    grad_a, send_a, grad_bias_a = back_sum_weight(
        core, scaled, t_own, near, far, slope, averaged_one, 0, None, sent
    )
    grad_b, send_b, _, extra = back_sum_weight(
        core, scaled, t_own, near, far, slope, averaged_one, 1, [grad_bias_a, bias_a, bias_b]
    )
    keep = weight_half(core, averaged_one, [grad_a, grad_b], False, extra, [], 8)
    orders_one = ("yxz", "zxyz")
    one = [PartSum(s, k, order) for s, k, order in zip((send_a, send_b), keep, orders_one)]
    sent = advance(one) + advance(two)
    scaled, ends, token = back_product([grad_a, grad_b], weight_one, inverse, t_halo, sent)
    near, far = exchange(ends[:BAND], ends[BAND:])

    sent = advance(one, token[0])
    advance(two, token[0])
    advance(one)
    sent = advance(one)
    grad_input, token = back_sum(core, scaled, t_own, near, far, sent)
    while one[0].todo:
        advance(two, token[0])
        advance(one, token[0])
    grad_two = jnp.concatenate([part.result() for part in two], axis=1)
    grad_one, biases = finish(one)
    return activations[None], grad_input[None], grad_one, biases[0], grad_two, biases[1]


def solution(mesh):
    rows = P("grp", "blk", None)
    spread = ("blk", "grp")
    return jax.shard_map(
        local,
        mesh=mesh,
        in_specs=(rows, rows, P("grp", "blk"), P(), P(), P(), P(), rows),
        out_specs=(rows, rows, P(spread, None), P(spread), P(spread, None), P(spread)),
        check_vma=False,
    )
```

```python
import math

import jax
import jax.numpy as jnp
from jax import lax
from jax.experimental import pallas as pl
from jax.experimental.pallas import tpu as pltpu
from jax.sharding import PartitionSpec as P

BAND = 256
BF = jnp.bfloat16
F32 = jnp.float32
LANES = 128
STEP = 512
PARTS = 2
ROOM = 6 << 20
VALUES = 12 << 20
SCALE = 0.7978845608
CUBIC = 0.044715


def dot(a, b, contract=((1,), (0,))):
    return lax.dot_general(a, b, (contract, ((), ())), preferred_element_type=F32)


def sds(shape, dtype):
    return jax.ShapeDtypeStruct(shape, dtype)


def call(body, steps, in_specs, out_specs, out_shape, flops, scratch=(), prefetch=0, after=()):
    inputs = prefetch + len(in_specs)
    specs = list(in_specs) + [pl.BlockSpec(memory_space=pl.ANY)] * len(after)

    def kernel(*refs):
        body(*refs[:inputs], *refs[inputs + len(after) :])

    def run(*args):
        several = isinstance(out_shape, list)
        outs = zip(out_specs, out_shape) if several else [(out_specs, out_shape)]
        need = ROOM
        for spec, array in [*zip(in_specs, args[prefetch:]), *outs]:
            if spec.block_shape is not None:
                copies = 1 if spec.pipeline_mode is not None else 2
                need += copies * math.prod(spec.block_shape) * array.dtype.itemsize
        need += sum(math.prod(ref.shape) * jnp.dtype(ref.dtype).itemsize for ref in scratch)
        return pl.pallas_call(
            kernel,
            grid_spec=pltpu.PrefetchScalarGridSpec(
                num_scalar_prefetch=prefetch,
                grid=(steps,),
                in_specs=specs,
                out_specs=out_specs,
                scratch_shapes=scratch,
            ),
            out_shape=out_shape,
            compiler_params=pltpu.CompilerParams(vmem_limit_bytes=need),
            cost_estimate=pl.CostEstimate(flops=flops, bytes_accessed=1 << 12, transcendentals=0),
        )(*args, *after)

    return run


def full(shape):
    pick = lambda j, *_: (0,) * len(shape)
    return pl.BlockSpec(shape, pick, pipeline_mode=pl.Buffered(1))


def cols(rows, base=0, count=None, width=STEP, start=0):
    if count is None:
        return pl.BlockSpec((rows, width), lambda j, *_: (0, start + j))
    return pl.BlockSpec((rows, width), lambda j, *_: (0, jnp.clip(j - base, 0, count - 1)))


WHOLE = pl.BlockSpec(memory_space=pltpu.VMEM)
SCALAR = pl.BlockSpec(memory_space=pltpu.SMEM)
ANY = pl.BlockSpec(memory_space=pl.ANY)


def whole_call(body, in_specs, out_specs, out_shape, flops, scratch=(), after=()):
    inputs = len(in_specs)

    def kernel(*refs):
        body(*refs[:inputs], *refs[inputs + len(after) :])

    held = sum(
        math.prod(ref.shape) * jnp.dtype(ref.dtype).itemsize
        for ref in scratch
        if ref.memory_space == pltpu.VMEM
    )
    made = pl.pallas_call(
        kernel,
        in_specs=list(in_specs) + [ANY] * len(after),
        out_specs=out_specs,
        out_shape=out_shape,
        scratch_shapes=scratch,
        compiler_params=pltpu.CompilerParams(vmem_limit_bytes=VALUES + held),
        cost_estimate=pl.CostEstimate(flops=flops, bytes_accessed=1 << 12, transcendentals=0),
    )
    return lambda *args: made(*args, *after)


def blocks(width, step=STEP):
    return [slice(at, at + step) for at in range(0, width, step)]


def count_own(core, slots, degree, field):
    nodes, slot_total = slots.shape
    width = field.shape[1]
    quarter = (nodes + 2 * BAND) // 4
    groups, steps = nodes // LANES, width // STEP
    pieces = LANES // 8

    def count(core_ref, slots_ref, degree_ref, t_own, t_halo, n_own, n_halo, key_ref, value_ref):
        group = pl.program_id(0)
        slot = slots_ref[...]
        q = (
            (slot >= quarter).astype(jnp.int32)
            + (slot >= 2 * quarter).astype(jnp.int32)
            + (slot >= 3 * quarter).astype(jnp.int32)
        )
        used = lax.broadcasted_iota(jnp.int32, slot.shape, 0) < degree_ref[...]
        key_ref[...] = slot - q * quarter
        value_ref[...] = jnp.where(used, jnp.left_shift(1, q * 8), 0)
        sub = lax.broadcasted_iota(jnp.int32, (8, LANES), 0)
        row = lax.broadcasted_iota(jnp.int32, (LANES, LANES), 0)
        col = lax.broadcasted_iota(jnp.int32, (LANES, LANES), 1)
        nodes_at = pl.ds(pl.multiple_of(group * LANES, LANES), LANES)
        for part in range(quarter // LANES):

            def add_slot(k, packed):
                key = jnp.broadcast_to(key_ref[pl.ds(k, 1), :], (8, LANES)) - sub
                value = jnp.broadcast_to(value_ref[pl.ds(k, 1), :], (8, LANES))
                return tuple(
                    acc + jnp.where(key == part * LANES + 8 * i, value, 0)
                    for i, acc in enumerate(packed)
                )

            packed = lax.fori_loop(
                0,
                slot_total,
                add_slot,
                tuple(jnp.zeros((8, LANES), jnp.int32) for _ in range(pieces)),
                unroll=4,
            )
            packed = jnp.concatenate(packed, axis=0)
            for q in range(4):
                counts = jnp.bitwise_and(jnp.right_shift(packed, 8 * q), 255)
                start = q * quarter + part * LANES
                own = start - BAND
                if 0 <= own < nodes:
                    counts = counts + jnp.where(row + own == col + group * LANES, 2, 0)
                    counts = counts.astype(F32)
                    t_own[own : own + LANES, :] = counts.astype(BF)
                    n_own[nodes_at, own : own + LANES] = counts.T.astype(BF)
                else:
                    after = own >= 0
                    inner = start - nodes - BAND if after else start
                    slot_of = core_ref[0] if after else 1 - core_ref[0]
                    at = pl.ds(pl.multiple_of(slot_of * BAND + inner, LANES), LANES)
                    counts = counts.astype(F32)
                    t_halo[at, :] = counts.astype(BF)
                    n_halo[nodes_at, at] = counts.T.astype(BF)

    def body(core_ref, slots_ref, degree_ref, f_ref, t_own, t_halo, n_own, n_halo, out, *scratch):
        step = pl.program_id(0)

        @pl.when(step < groups)
        def _():
            count(core_ref, slots_ref, degree_ref, t_own, t_halo, n_own, n_halo, *scratch)

        @pl.when(step >= groups)
        def _():
            out[...] = dot(n_own[...], f_ref[...]).astype(BF)

    tall = lambda h: cols(h, 0, groups, LANES)
    return call(
        body,
        groups + steps,
        [tall(slot_total), tall(1), cols(nodes, groups, steps)],
        [
            tall(nodes),
            tall(2 * BAND),
            full((nodes, nodes)),
            full((nodes, 2 * BAND)),
            cols(nodes, groups, steps),
        ],
        [
            sds((nodes, nodes), BF),
            sds((2 * BAND, nodes), BF),
            sds((nodes, nodes), BF),
            sds((nodes, 2 * BAND), BF),
            sds((nodes, width), BF),
        ],
        flops=20 << 30,
        scratch=[pltpu.VMEM((slot_total, LANES), jnp.int32)] * 2,
        prefetch=1,
    )(core, slots.T, degree[None, :], field)


def own_sum(n_own, field):
    def body(n_ref, f_ref, out):
        for at in blocks(width):
            out[:, at] = dot(n_ref[...], f_ref[:, at]).astype(BF)

    nodes, width = field.shape
    return whole_call(
        body,
        [WHOLE] * 2,
        WHOLE,
        sds((nodes, width), BF),
        flops=16 * nodes * nodes * width,
    )(n_own, field)


def gelu_parts(p):
    square = p * p
    half = 0.5 + 0.5 * jnp.tanh(p * (SCALE + SCALE * CUBIC * square))
    value = p * half
    return value, half + (value - value * half) * (2.0 * SCALE + 6.0 * SCALE * CUBIC * square)


def layer(core, own, n_halo, near, far, inverse, weight, bias, cotangent=None):
    last = cotangent is not None
    nodes, width = own.shape
    grads = PARTS if last else 1

    def body(core_ref, own_ref, n_ref, near_ref, far_ref, inv_ref, w_ref, b_ref, *refs):
        c_ref = refs[0] if last else None
        out_t, out, *refs = refs[1:] if last else refs
        if not last:
            to_near, to_far, *refs = refs
        out_grads, (avg, *rest) = refs[:grads], refs[grads:]
        for at in blocks(width):
            total = own_ref[:, at].astype(F32) + dot(n_ref[:, :BAND], near_ref[:, at])
            total = (total + dot(n_ref[:, BAND:], far_ref[:, at])) * inv_ref[...]
            avg[:, at] = total.astype(BF)
            out_t[at, :] = total.T.astype(BF)
        copies = []
        for i, at in enumerate(blocks(width)):
            value, grad = gelu_parts(dot(avg[...], w_ref[:, at]) + b_ref[:, at])
            if last:
                made, sems = rest
                made[:, at] = value.astype(BF)
                copies.append(pltpu.make_async_copy(made.at[:, at], out.at[:, at], sems.at[i]))
                copies[-1].start()
                grad = c_ref[:, at].astype(F32) * grad
            else:
                out[:, at] = value.astype(BF)
            part, k = divmod(at.start, width // grads)
            out_grads[part][:, k : k + STEP] = grad.astype(BF)
        if not last:
            end = nodes - BAND
            for to, at in ((to_near, (1 - core_ref[0]) * end), (to_far, core_ref[0] * end)):
                to[...] = out[pl.ds(pl.multiple_of(at, BAND), BAND), :]
        for copy in copies:
            copy.wait()

    scratch = [pltpu.VMEM((nodes, width), BF)]
    if last:
        scratch += [pltpu.VMEM((nodes, width), BF), pltpu.SemaphoreType.DMA((width // STEP,))]
    return whole_call(
        body,
        [SCALAR] + [WHOLE] * (7 + last),
        [WHOLE, ANY if last else WHOLE] + [WHOLE] * (2 if last else 3),
        [sds((width, nodes), BF), sds((nodes, width), BF)]
        + ([] if last else [sds((BAND, width), BF)] * 2)
        + [sds((nodes, width // grads), BF)] * grads,
        flops=2 * nodes * width * (2 * BAND + width),
        scratch=scratch,
    )(core, own, n_halo, near, far, inverse, weight, bias, *([cotangent] if last else []))


def back_product(grad_pre, weight, inverse, t_halo, after=()):
    nodes, width = grad_pre[0].shape[0], weight.shape[1]
    count = len(grad_pre)

    def body(*refs):
        g_refs, (w_ref, inv_ref, t_ref, scaled, ends, token) = refs[:count], refs[count:]
        token[0] = 0
        for at in blocks(width):
            total, k = None, 0
            for g_ref in g_refs:
                size = g_ref.shape[1]
                part = dot(g_ref[...], w_ref[at, k : k + size], ((1,), (1,)))
                total = part if total is None else total + part
                k += size
            value = (total * inv_ref[...]).astype(BF)
            scaled[:, at] = value
            ends[:, at] = dot(t_ref[...], value).astype(BF)

    return whole_call(
        body,
        [WHOLE] * (count + 3),
        [WHOLE, WHOLE, SCALAR],
        [sds((nodes, width), BF), sds((2 * BAND, width), BF), sds((1,), jnp.int32)],
        flops=2 * nodes * width * (width + 2 * BAND),
        after=after,
    )(*grad_pre, weight, inverse, t_halo)


def back_sum_step(core_ref, s_ref, t_ref, near_ref, far_ref, slope_ref, at):
    nodes = t_ref.shape[0]
    total = dot(t_ref[...], s_ref[:, at])
    near, far = near_ref[:, at].astype(F32), far_ref[:, at].astype(F32)
    odd = core_ref[0] == 1
    pieces = (
        (0, BAND, total[:BAND] + jnp.where(odd, near, far)),
        (BAND, nodes - BAND, total[BAND : nodes - BAND]),
        (nodes - BAND, nodes, total[nodes - BAND :] + jnp.where(odd, far, near)),
    )
    for lo, hi, value in pieces:
        if slope_ref is not None:
            value = value * slope_ref[lo:hi, at].astype(F32)
        yield lo, hi, value.astype(BF)


def back_sum(core, scaled, t_own, near, far, after=()):
    nodes, width = scaled.shape

    def body(core_ref, s_ref, t_ref, near_ref, far_ref, out, token, made, sems):
        token[0] = 0
        copies = []
        for i, at in enumerate(blocks(width)):
            for lo, hi, value in back_sum_step(
                core_ref, s_ref, t_ref, near_ref, far_ref, None, at
            ):
                made[lo:hi, at] = value
            copies.append(pltpu.make_async_copy(made.at[:, at], out.at[:, at], sems.at[i]))
            copies[-1].start()
        for copy in copies:
            copy.wait()

    return whole_call(
        body,
        [SCALAR] + [WHOLE] * 4,
        [ANY, SCALAR],
        [sds((nodes, width), BF), sds((1,), jnp.int32)],
        flops=0,
        scratch=[pltpu.VMEM((nodes, width), BF), pltpu.SemaphoreType.DMA((width // STEP,))],
        after=after,
    )(core, scaled, t_own, near, far)


def half_rows(a_ref, which):
    picked = a_ref[:, which]
    return picked.reshape(picked.shape[0] * picked.shape[1], picked.shape[2])


def by_core(rows):
    blk = lax.axis_size("blk")
    return rows.reshape(blk // 2, 2, rows.shape[0] // blk, rows.shape[1])


def weight_half(core, averaged_t, grad_pre, flip, extra=None, after=(), weigh=1):
    view = by_core(averaged_t)
    nodes = grad_pre[0].shape[0]
    half = averaged_t.shape[0] // 2
    count = len(grad_pre)
    more = [] if extra is None else [by_core(extra)]

    def body(core_ref, a_ref, *refs):
        g_refs, refs = refs[:count], refs[count:]
        e_refs, outs, bias = refs[: len(more)], refs[len(more) :][:count], refs[len(more) + count :]
        which = 1 - core_ref[0] if flip else core_ref[0]
        rows = half_rows(a_ref, which)
        for i, (g_ref, out) in enumerate(zip(g_refs, outs)):
            for at in blocks(g_ref.shape[1]):
                out[:, at] = dot(rows, g_ref[:, at]).astype(BF)
            if flip:
                bias[i][...] = jnp.sum(g_ref[...].astype(F32), axis=0, keepdims=True)
        for e_ref in e_refs:
            outs[-1][:, g_refs[-1].shape[1] :] = half_rows(e_ref, which)

    widths = [g.shape[1] for g in grad_pre]
    shapes = [sds((half, w), BF) for w in widths]
    if more:
        shapes[-1] = sds((half, widths[-1] + extra.shape[1]), BF)
    return whole_call(
        body,
        [SCALAR] + [WHOLE] * (1 + count + len(more)),
        [WHOLE] * (count * (1 + flip)),
        shapes + [sds((1, w), F32) for w in widths] * flip,
        flops=2 * nodes * half * sum(widths) * weigh,
        after=after,
    )(core, view, *grad_pre, *more)


def back_sum_weight(core, scaled, t_own, near, far, slope, averaged_t, part, biases=None, after=()):
    nodes, width = scaled.shape
    whole = width
    width //= PARTS
    view = by_core(averaged_t)
    half = averaged_t.shape[0] // 2
    start = part * width
    given = [] if biases is None else list(biases)

    def body(core_ref, s_ref, t_ref, near_ref, far_ref, p_ref, a_ref, *refs):
        given_refs, (grad_pre, send, bias, *rest) = refs[: len(given)], refs[len(given) :]
        rows = half_rows(a_ref, 1 - core_ref[0])
        for out_at, at in zip(blocks(width), blocks(whole)[start // STEP :]):
            for lo, hi, value in back_sum_step(
                core_ref, s_ref, t_ref, near_ref, far_ref, p_ref, at
            ):
                grad_pre[lo:hi, out_at] = value
            grad = grad_pre[:, out_at]
            bias[:, out_at] = jnp.sum(grad.astype(F32), axis=0, keepdims=True)
            send[:, out_at] = dot(rows, grad).astype(BF)
        if given:
            one, two = [*given_refs[:part], bias], given_refs[part:]
            lane = lax.broadcasted_iota(jnp.int32, (LANES, LANES), 1)
            spread = rest[1]
            for at in blocks(whole, LANES):
                columns = []
                for refs in (one, two):
                    size = refs[0].shape[1]
                    ref, k = refs[at.start // size], at.start % size
                    columns.append(jnp.broadcast_to(ref[:, k : k + LANES], (LANES, LANES)).T)
                mixed = jnp.where(lane < LANES // 2, *columns).astype(BF)
                rest[0][at, :] = mixed
                spread[at, :] = mixed
            run = view.shape[2]
            picked = spread.reshape(whole // (2 * run), 2, run, LANES)
            send[:, width:] = half_rows(picked, 1 - core_ref[0])

    columns = width + (LANES if given else 0)
    shapes = [sds((nodes, width), BF), sds((half, columns), BF), sds((1, width), F32)]
    return whole_call(
        body,
        [SCALAR] + [WHOLE] * (6 + len(given)),
        [WHOLE] * (3 + bool(given)),
        shapes + [sds((whole, LANES), BF)] * bool(given),
        flops=2 * nodes * width * (nodes + half),
        scratch=[pltpu.VMEM((whole, LANES), BF)] * bool(given),
        after=after,
    )(core, scaled, t_own, near, far, slope, view, *given)


def swap(axis, distance):
    return [(i, i ^ distance) for i in range(lax.axis_size(axis))]


def exchange(near, far):
    count = lax.axis_size("blk")
    other = [(i, (i + 1 if i % 2 else i - 1) % count) for i in range(count)]
    return lax.ppermute(near, "blk", swap("blk", 1)), lax.ppermute(far, "blk", other)


def field_halo(field):
    nodes = field.shape[0]
    odd = lax.axis_index("blk") % 2
    rows = lambda last: lax.dynamic_slice_in_dim(field, last * (nodes - BAND), BAND, 0)
    return exchange(rows(1 - odd), rows(odd))


def place_bits():
    b, g = lax.axis_index("blk"), lax.axis_index("grp")
    line = (lax.axis_size("blk") // 4).bit_length() - 1
    across = lax.axis_size("grp").bit_length() - 1
    bits = [(b // (4 << i)) % 2 for i in reversed(range(line))] + [(b // 2) % 2]
    return bits + [(g // (1 << i)) % 2 for i in reversed(range(across))]


def steps_of(axis):
    line = (lax.axis_size("blk") // 4).bit_length() - 1
    across = lax.axis_size("grp").bit_length() - 1
    if axis == "y":
        return [(line, "blk", 2)]
    if axis == "x":
        return [(line + 1 + i, "grp", 1 << (across - 1 - i)) for i in range(across)]
    return [(line - 1 - axis, "blk", 4 << axis)] if axis < line else []


class PartSum:
    def __init__(self, send, keep, order):
        self.bits = place_bits()
        terms = [keep, lax.ppermute(send, "blk", swap("blk", 1))]
        self.terms = [t.reshape((2,) * len(self.bits) + (-1, t.shape[-1])) for t in terms]
        self.todo = [step for axis in orders(order) for step in steps_of(axis)]
        self.settled = []

    def sum(self, flip=None, token=0):
        total = 0.0
        for term in self.terms:
            at, sizes = [], []
            for dim, bit in enumerate(self.bits):
                pick = term.shape[dim] == 2 and dim in self.settled
                at.append((1 - bit if dim == flip else bit) + token if pick else 0)
                sizes.append(1 if pick else term.shape[dim])
            total = total + lax.dynamic_slice(
                term, (*at, 0, 0), (*sizes, *term.shape[-2:])
            ).astype(F32)
        return total

    def step(self, token=0):
        dim, axis, distance = self.todo.pop(0)
        self.settled.append(dim)
        sent = self.sum(dim, token).astype(BF)
        self.terms = self.terms + [lax.ppermute(sent, axis, swap(axis, distance))]
        return sent

    def before_last(self):
        *self.terms, _ = self.terms
        return self.sum().reshape(self.terms[0].shape[-2:])

    def result(self):
        while self.todo:
            self.step()
        return self.sum().reshape(self.terms[0].shape[-2:])


def joint_step(parts, token=0):
    dim, axis, distance = parts[0].todo[0]
    sent = []
    for part in parts:
        part.todo.pop(0)
        part.settled.append(dim)
        sent.append(part.sum(dim, token).astype(BF))
    sent = jnp.concatenate(sent, axis=-1)
    received = lax.ppermute(sent, axis, swap(axis, distance))
    at = 0
    for part in parts:
        width = part.terms[0].shape[-1]
        part.terms = part.terms + [received[..., at : at + width]]
        at += width
        part.last = received
    return sent


def advance(parts, token=0):
    if not parts[0].todo:
        return []
    if len(parts) > 1 and all(part.todo == parts[0].todo for part in parts):
        return [joint_step(parts, token)]
    return [part.step(token) for part in parts]


def finish(parts):
    received = parts[0].last.reshape(-1, parts[0].last.shape[-1])
    sums = [part.before_last() for part in parts]
    rows = received.shape[0]
    width = received.shape[1] - LANES

    def body(*refs):
        *sum_refs, last_ref, out, bias_one, bias_two = refs
        at = 0
        for ref in sum_refs:
            to = min(at + ref.shape[1], width)
            out[:, at:to] = ref[:, : to - at] + last_ref[:, at:to].astype(F32)
            at = to
        tile = (sum_refs[-1][:, -LANES:] + last_ref[:, width:].astype(F32)).T
        bias_one[...] = tile[:1]
        bias_two[...] = tile[LANES // 2 : LANES // 2 + 1]

    out, bias_one, bias_two = whole_call(
        body,
        [WHOLE] * (1 + len(sums)),
        [WHOLE] * 3,
        [sds((rows, width), F32), sds((1, rows), F32), sds((1, rows), F32)],
        flops=0,
    )(*sums, received)
    return out, [bias_one[0], bias_two[0]]


def orders(kind):
    rest = range(1, (lax.axis_size("blk") // 4).bit_length() - 1)
    return {
        "xyz": ["x", "y", 0, *rest],
        "yxz": ["y", "x", 0, *rest],
        "zxyz": [0, "x", "y", *rest],
        "xzyz": ["x", 0, "y", *rest],
        "yzxz": ["y", 0, "x", *rest],
        "zyxz": [0, "y", "x", *rest],
    }[kind]


def local(features, neighbours, degree, weight_one, bias_one, weight_two, bias_two, cotangent):
    core = (lax.axis_index("blk") % 2).reshape(1).astype(jnp.int32)
    inverse = 1.0 / (degree[0].astype(F32)[:, None] + 1.0)
    field = features[0]
    width = field.shape[1]

    near, far = field_halo(field)
    t_own, t_halo, n_own, n_halo, own = count_own(core, neighbours[0], degree[0], field)
    averaged_one, hidden, near, far, slope = layer(
        core, own, n_halo, near, far, inverse, weight_one, bias_one[None, :]
    )
    near, far = exchange(near, far)
    own = own_sum(n_own, hidden)
    averaged_two, activations, *halves = layer(
        core, own, n_halo, near, far, inverse, weight_two, bias_two[None, :], cotangent[0]
    )
    scaled, ends, _ = back_product(halves, weight_two, inverse, t_halo)
    near, far = exchange(ends[:BAND], ends[BAND:])

    *send, bias_a, bias_b = weight_half(core, averaged_two, halves, True)
    keep = weight_half(core, averaged_two, halves, False, None, send, 8)
    two = [PartSum(a, b, kind) for a, b, kind in zip(send, keep, ("xzyz","zxyz"))]
    sent = advance(two)

    grad_a, send_a, grad_bias_a = back_sum_weight(
        core, scaled, t_own, near, far, slope, averaged_one, 0, None, sent
    )
    grad_b, send_b, _, extra = back_sum_weight(
        core, scaled, t_own, near, far, slope, averaged_one, 1, [grad_bias_a, bias_a, bias_b]
    )
    keep = weight_half(core, averaged_one, [grad_a, grad_b], False, extra, [], 8)
    orders_one = ("yxz", "zxyz")
    one = [PartSum(s, k, order) for s, k, order in zip((send_a, send_b), keep, orders_one)]
    sent = advance(one) + advance(two)
    scaled, ends, token = back_product([grad_a, grad_b], weight_one, inverse, t_halo, sent)
    near, far = exchange(ends[:BAND], ends[BAND:])

    sent = advance(one, token[0])
    advance(two, token[0])
    advance(one)
    sent = advance(one)
    grad_input, token = back_sum(core, scaled, t_own, near, far, sent)
    while one[0].todo:
        advance(two, token[0])
        advance(one, token[0])
    grad_two = jnp.concatenate([part.result() for part in two], axis=1)
    grad_one, biases = finish(one)
    return activations[None], grad_input[None], grad_one, biases[0], grad_two, biases[1]


def solution(mesh):
    rows = P("grp", "blk", None)
    spread = ("blk", "grp")
    return jax.shard_map(
        local,
        mesh=mesh,
        in_specs=(rows, rows, P("grp", "blk"), P(), P(), P(), P(), rows),
        out_specs=(rows, rows, P(spread, None), P(spread), P(spread, None), P(spread)),
        check_vma=False,
    )
```

```python
import math

import jax
import jax.numpy as jnp
from jax import lax
from jax.experimental import pallas as pl
from jax.experimental.pallas import tpu as pltpu
from jax.sharding import PartitionSpec as P

BAND = 256
BF = jnp.bfloat16
F32 = jnp.float32
LANES = 128
STEP = 512
PARTS = 2
ROOM = 6 << 20
VALUES = 12 << 20
SCALE = 0.7978845608
CUBIC = 0.044715


def dot(a, b, contract=((1,), (0,))):
    return lax.dot_general(a, b, (contract, ((), ())), preferred_element_type=F32)


def sds(shape, dtype):
    return jax.ShapeDtypeStruct(shape, dtype)


def call(body, steps, in_specs, out_specs, out_shape, flops, scratch=(), prefetch=0, after=()):
    inputs = prefetch + len(in_specs)
    specs = list(in_specs) + [pl.BlockSpec(memory_space=pl.ANY)] * len(after)

    def kernel(*refs):
        body(*refs[:inputs], *refs[inputs + len(after) :])

    def run(*args):
        several = isinstance(out_shape, list)
        outs = zip(out_specs, out_shape) if several else [(out_specs, out_shape)]
        need = ROOM
        for spec, array in [*zip(in_specs, args[prefetch:]), *outs]:
            if spec.block_shape is not None:
                copies = 1 if spec.pipeline_mode is not None else 2
                need += copies * math.prod(spec.block_shape) * array.dtype.itemsize
        need += sum(math.prod(ref.shape) * jnp.dtype(ref.dtype).itemsize for ref in scratch)
        return pl.pallas_call(
            kernel,
            grid_spec=pltpu.PrefetchScalarGridSpec(
                num_scalar_prefetch=prefetch,
                grid=(steps,),
                in_specs=specs,
                out_specs=out_specs,
                scratch_shapes=scratch,
            ),
            out_shape=out_shape,
            compiler_params=pltpu.CompilerParams(vmem_limit_bytes=need),
            cost_estimate=pl.CostEstimate(flops=flops, bytes_accessed=1 << 12, transcendentals=0),
        )(*args, *after)

    return run


def full(shape):
    pick = lambda j, *_: (0,) * len(shape)
    return pl.BlockSpec(shape, pick, pipeline_mode=pl.Buffered(1))


def cols(rows, base=0, count=None, width=STEP, start=0):
    if count is None:
        return pl.BlockSpec((rows, width), lambda j, *_: (0, start + j))
    return pl.BlockSpec((rows, width), lambda j, *_: (0, jnp.clip(j - base, 0, count - 1)))


WHOLE = pl.BlockSpec(memory_space=pltpu.VMEM)
SCALAR = pl.BlockSpec(memory_space=pltpu.SMEM)
ANY = pl.BlockSpec(memory_space=pl.ANY)


def whole_call(body, in_specs, out_specs, out_shape, flops, scratch=(), after=()):
    inputs = len(in_specs)

    def kernel(*refs):
        body(*refs[:inputs], *refs[inputs + len(after) :])

    held = sum(
        math.prod(ref.shape) * jnp.dtype(ref.dtype).itemsize
        for ref in scratch
        if ref.memory_space == pltpu.VMEM
    )
    made = pl.pallas_call(
        kernel,
        in_specs=list(in_specs) + [ANY] * len(after),
        out_specs=out_specs,
        out_shape=out_shape,
        scratch_shapes=scratch,
        compiler_params=pltpu.CompilerParams(vmem_limit_bytes=VALUES + held),
        cost_estimate=pl.CostEstimate(flops=flops, bytes_accessed=1 << 12, transcendentals=0),
    )
    return lambda *args: made(*args, *after)


def blocks(width, step=STEP):
    return [slice(at, at + step) for at in range(0, width, step)]


def count_own(core, slots, degree, field):
    nodes, slot_total = slots.shape
    width = field.shape[1]
    quarter = (nodes + 2 * BAND) // 4
    groups, steps = nodes // LANES, width // STEP
    pieces = LANES // 8

    def count(core_ref, slots_ref, degree_ref, t_own, t_halo, n_own, n_halo, key_ref, value_ref):
        group = pl.program_id(0)
        slot = slots_ref[...]
        q = (
            (slot >= quarter).astype(jnp.int32)
            + (slot >= 2 * quarter).astype(jnp.int32)
            + (slot >= 3 * quarter).astype(jnp.int32)
        )
        used = lax.broadcasted_iota(jnp.int32, slot.shape, 0) < degree_ref[...]
        key_ref[...] = slot - q * quarter
        value_ref[...] = jnp.where(used, jnp.left_shift(1, q * 8), 0)
        sub = lax.broadcasted_iota(jnp.int32, (8, LANES), 0)
        row = lax.broadcasted_iota(jnp.int32, (LANES, LANES), 0)
        col = lax.broadcasted_iota(jnp.int32, (LANES, LANES), 1)
        nodes_at = pl.ds(pl.multiple_of(group * LANES, LANES), LANES)
        for part in range(quarter // LANES):

            def add_slot(k, packed):
                key = jnp.broadcast_to(key_ref[pl.ds(k, 1), :], (8, LANES)) - sub
                value = jnp.broadcast_to(value_ref[pl.ds(k, 1), :], (8, LANES))
                return tuple(
                    acc + jnp.where(key == part * LANES + 8 * i, value, 0)
                    for i, acc in enumerate(packed)
                )

            packed = lax.fori_loop(
                0,
                slot_total,
                add_slot,
                tuple(jnp.zeros((8, LANES), jnp.int32) for _ in range(pieces)),
                unroll=4,
            )
            packed = jnp.concatenate(packed, axis=0)
            for q in range(4):
                counts = jnp.bitwise_and(jnp.right_shift(packed, 8 * q), 255)
                start = q * quarter + part * LANES
                own = start - BAND
                if 0 <= own < nodes:
                    counts = counts + jnp.where(row + own == col + group * LANES, 2, 0)
                    counts = counts.astype(F32)
                    t_own[own : own + LANES, :] = counts.astype(BF)
                    n_own[nodes_at, own : own + LANES] = counts.T.astype(BF)
                else:
                    after = own >= 0
                    inner = start - nodes - BAND if after else start
                    slot_of = core_ref[0] if after else 1 - core_ref[0]
                    at = pl.ds(pl.multiple_of(slot_of * BAND + inner, LANES), LANES)
                    counts = counts.astype(F32)
                    t_halo[at, :] = counts.astype(BF)
                    n_halo[nodes_at, at] = counts.T.astype(BF)

    def body(core_ref, slots_ref, degree_ref, f_ref, t_own, t_halo, n_own, n_halo, out, *scratch):
        step = pl.program_id(0)

        @pl.when(step < groups)
        def _():
            count(core_ref, slots_ref, degree_ref, t_own, t_halo, n_own, n_halo, *scratch)

        @pl.when(step >= groups)
        def _():
            out[...] = dot(n_own[...], f_ref[...]).astype(BF)

    tall = lambda h: cols(h, 0, groups, LANES)
    return call(
        body,
        groups + steps,
        [tall(slot_total), tall(1), cols(nodes, groups, steps)],
        [
            tall(nodes),
            tall(2 * BAND),
            full((nodes, nodes)),
            full((nodes, 2 * BAND)),
            cols(nodes, groups, steps),
        ],
        [
            sds((nodes, nodes), BF),
            sds((2 * BAND, nodes), BF),
            sds((nodes, nodes), BF),
            sds((nodes, 2 * BAND), BF),
            sds((nodes, width), BF),
        ],
        flops=20 << 30,
        scratch=[pltpu.VMEM((slot_total, LANES), jnp.int32)] * 2,
        prefetch=1,
    )(core, slots.T, degree[None, :], field)


def own_sum(n_own, field):
    def body(n_ref, f_ref, out):
        for at in blocks(width):
            out[:, at] = dot(n_ref[...], f_ref[:, at]).astype(BF)

    nodes, width = field.shape
    return whole_call(
        body,
        [WHOLE] * 2,
        WHOLE,
        sds((nodes, width), BF),
        flops=16 * nodes * nodes * width,
    )(n_own, field)


def gelu_parts(p):
    square = p * p
    half = 0.5 + 0.5 * jnp.tanh(p * (SCALE + SCALE * CUBIC * square))
    value = p * half
    return value, half + (value - value * half) * (2.0 * SCALE + 6.0 * SCALE * CUBIC * square)


def layer(core, own, n_halo, near, far, inverse, weight, bias, cotangent=None):
    last = cotangent is not None
    nodes, width = own.shape
    grads = PARTS if last else 1

    def body(core_ref, own_ref, n_ref, near_ref, far_ref, inv_ref, w_ref, b_ref, *refs):
        c_ref = refs[0] if last else None
        out_t, out, *refs = refs[1:] if last else refs
        if not last:
            to_near, to_far, *refs = refs
        out_grads, (avg, *rest) = refs[:grads], refs[grads:]
        for at in blocks(width):
            total = own_ref[:, at].astype(F32) + dot(n_ref[:, :BAND], near_ref[:, at])
            total = (total + dot(n_ref[:, BAND:], far_ref[:, at])) * inv_ref[...]
            avg[:, at] = total.astype(BF)
            out_t[at, :] = total.T.astype(BF)
        copies = []
        for i, at in enumerate(blocks(width)):
            value, grad = gelu_parts(dot(avg[...], w_ref[:, at]) + b_ref[:, at])
            if last:
                made, sems = rest
                made[:, at] = value.astype(BF)
                copies.append(pltpu.make_async_copy(made.at[:, at], out.at[:, at], sems.at[i]))
                copies[-1].start()
                grad = c_ref[:, at].astype(F32) * grad
            else:
                out[:, at] = value.astype(BF)
            part, k = divmod(at.start, width // grads)
            out_grads[part][:, k : k + STEP] = grad.astype(BF)
        if not last:
            end = nodes - BAND
            for to, at in ((to_near, (1 - core_ref[0]) * end), (to_far, core_ref[0] * end)):
                to[...] = out[pl.ds(pl.multiple_of(at, BAND), BAND), :]
        for copy in copies:
            copy.wait()

    scratch = [pltpu.VMEM((nodes, width), BF)]
    if last:
        scratch += [pltpu.VMEM((nodes, width), BF), pltpu.SemaphoreType.DMA((width // STEP,))]
    return whole_call(
        body,
        [SCALAR] + [WHOLE] * (7 + last),
        [WHOLE, ANY if last else WHOLE] + [WHOLE] * (2 if last else 3),
        [sds((width, nodes), BF), sds((nodes, width), BF)]
        + ([] if last else [sds((BAND, width), BF)] * 2)
        + [sds((nodes, width // grads), BF)] * grads,
        flops=0,
        scratch=scratch,
    )(core, own, n_halo, near, far, inverse, weight, bias, *([cotangent] if last else []))


def back_product(grad_pre, weight, inverse, t_halo, after=()):
    nodes, width = grad_pre[0].shape[0], weight.shape[1]
    count = len(grad_pre)

    def body(*refs):
        g_refs, (w_ref, inv_ref, t_ref, scaled, ends, token) = refs[:count], refs[count:]
        token[0] = 0
        for at in blocks(width):
            total, k = None, 0
            for g_ref in g_refs:
                size = g_ref.shape[1]
                part = dot(g_ref[...], w_ref[at, k : k + size], ((1,), (1,)))
                total = part if total is None else total + part
                k += size
            value = (total * inv_ref[...]).astype(BF)
            scaled[:, at] = value
            ends[:, at] = dot(t_ref[...], value).astype(BF)

    return whole_call(
        body,
        [WHOLE] * (count + 3),
        [WHOLE, WHOLE, SCALAR],
        [sds((nodes, width), BF), sds((2 * BAND, width), BF), sds((1,), jnp.int32)],
        flops=2 * nodes * width * (width + 2 * BAND),
        after=after,
    )(*grad_pre, weight, inverse, t_halo)


def back_sum_step(core_ref, s_ref, t_ref, near_ref, far_ref, slope_ref, at):
    nodes = t_ref.shape[0]
    total = dot(t_ref[...], s_ref[:, at])
    near, far = near_ref[:, at].astype(F32), far_ref[:, at].astype(F32)
    odd = core_ref[0] == 1
    pieces = (
        (0, BAND, total[:BAND] + jnp.where(odd, near, far)),
        (BAND, nodes - BAND, total[BAND : nodes - BAND]),
        (nodes - BAND, nodes, total[nodes - BAND :] + jnp.where(odd, far, near)),
    )
    for lo, hi, value in pieces:
        if slope_ref is not None:
            value = value * slope_ref[lo:hi, at].astype(F32)
        yield lo, hi, value.astype(BF)


def back_sum(core, scaled, t_own, near, far, after=()):
    nodes, width = scaled.shape

    def body(core_ref, s_ref, t_ref, near_ref, far_ref, out, token, made, sems):
        token[0] = 0
        copies = []
        for i, at in enumerate(blocks(width)):
            for lo, hi, value in back_sum_step(
                core_ref, s_ref, t_ref, near_ref, far_ref, None, at
            ):
                made[lo:hi, at] = value
            copies.append(pltpu.make_async_copy(made.at[:, at], out.at[:, at], sems.at[i]))
            copies[-1].start()
        for copy in copies:
            copy.wait()

    return whole_call(
        body,
        [SCALAR] + [WHOLE] * 4,
        [ANY, SCALAR],
        [sds((nodes, width), BF), sds((1,), jnp.int32)],
        flops=0,
        scratch=[pltpu.VMEM((nodes, width), BF), pltpu.SemaphoreType.DMA((width // STEP,))],
        after=after,
    )(core, scaled, t_own, near, far)


def half_rows(a_ref, which):
    picked = a_ref[:, which]
    return picked.reshape(picked.shape[0] * picked.shape[1], picked.shape[2])


def by_core(rows):
    blk = lax.axis_size("blk")
    return rows.reshape(blk // 2, 2, rows.shape[0] // blk, rows.shape[1])


def weight_half(core, averaged_t, grad_pre, flip, extra=None, after=(), weigh=1):
    view = by_core(averaged_t)
    nodes = grad_pre[0].shape[0]
    half = averaged_t.shape[0] // 2
    count = len(grad_pre)
    more = [] if extra is None else [by_core(extra)]

    def body(core_ref, a_ref, *refs):
        g_refs, refs = refs[:count], refs[count:]
        e_refs, outs, bias = refs[: len(more)], refs[len(more) :][:count], refs[len(more) + count :]
        which = 1 - core_ref[0] if flip else core_ref[0]
        rows = half_rows(a_ref, which)
        for i, (g_ref, out) in enumerate(zip(g_refs, outs)):
            for at in blocks(g_ref.shape[1]):
                out[:, at] = dot(rows, g_ref[:, at]).astype(BF)
            if flip:
                bias[i][...] = jnp.sum(g_ref[...].astype(F32), axis=0, keepdims=True)
        for e_ref in e_refs:
            outs[-1][:, g_refs[-1].shape[1] :] = half_rows(e_ref, which)

    widths = [g.shape[1] for g in grad_pre]
    shapes = [sds((half, w), BF) for w in widths]
    if more:
        shapes[-1] = sds((half, widths[-1] + extra.shape[1]), BF)
    return whole_call(
        body,
        [SCALAR] + [WHOLE] * (1 + count + len(more)),
        [WHOLE] * (count * (1 + flip)),
        shapes + [sds((1, w), F32) for w in widths] * flip,
        flops=2 * nodes * half * sum(widths) * weigh,
        after=after,
    )(core, view, *grad_pre, *more)


def back_sum_weight(core, scaled, t_own, near, far, slope, averaged_t, part, biases=None, after=()):
    nodes, width = scaled.shape
    whole = width
    width //= PARTS
    view = by_core(averaged_t)
    half = averaged_t.shape[0] // 2
    start = part * width
    given = [] if biases is None else list(biases)

    def body(core_ref, s_ref, t_ref, near_ref, far_ref, p_ref, a_ref, *refs):
        given_refs, (grad_pre, send, bias, *rest) = refs[: len(given)], refs[len(given) :]
        rows = half_rows(a_ref, 1 - core_ref[0])
        for out_at, at in zip(blocks(width), blocks(whole)[start // STEP :]):
            for lo, hi, value in back_sum_step(
                core_ref, s_ref, t_ref, near_ref, far_ref, p_ref, at
            ):
                grad_pre[lo:hi, out_at] = value
            grad = grad_pre[:, out_at]
            bias[:, out_at] = jnp.sum(grad.astype(F32), axis=0, keepdims=True)
            send[:, out_at] = dot(rows, grad).astype(BF)
        if given:
            one, two = [*given_refs[:part], bias], given_refs[part:]
            lane = lax.broadcasted_iota(jnp.int32, (LANES, LANES), 1)
            spread = rest[1]
            for at in blocks(whole, LANES):
                columns = []
                for refs in (one, two):
                    size = refs[0].shape[1]
                    ref, k = refs[at.start // size], at.start % size
                    columns.append(jnp.broadcast_to(ref[:, k : k + LANES], (LANES, LANES)).T)
                mixed = jnp.where(lane < LANES // 2, *columns).astype(BF)
                rest[0][at, :] = mixed
                spread[at, :] = mixed
            run = view.shape[2]
            picked = spread.reshape(whole // (2 * run), 2, run, LANES)
            send[:, width:] = half_rows(picked, 1 - core_ref[0])

    columns = width + (LANES if given else 0)
    shapes = [sds((nodes, width), BF), sds((half, columns), BF), sds((1, width), F32)]
    return whole_call(
        body,
        [SCALAR] + [WHOLE] * (6 + len(given)),
        [WHOLE] * (3 + bool(given)),
        shapes + [sds((whole, LANES), BF)] * bool(given),
        flops=2 * nodes * width * (nodes + half),
        scratch=[pltpu.VMEM((whole, LANES), BF)] * bool(given),
        after=after,
    )(core, scaled, t_own, near, far, slope, view, *given)


def swap(axis, distance):
    return [(i, i ^ distance) for i in range(lax.axis_size(axis))]


def exchange(near, far):
    count = lax.axis_size("blk")
    other = [(i, (i + 1 if i % 2 else i - 1) % count) for i in range(count)]
    return lax.ppermute(near, "blk", swap("blk", 1)), lax.ppermute(far, "blk", other)


def field_halo(field):
    nodes = field.shape[0]
    odd = lax.axis_index("blk") % 2
    rows = lambda last: lax.dynamic_slice_in_dim(field, last * (nodes - BAND), BAND, 0)
    return exchange(rows(1 - odd), rows(odd))


def place_bits():
    b, g = lax.axis_index("blk"), lax.axis_index("grp")
    line = (lax.axis_size("blk") // 4).bit_length() - 1
    across = lax.axis_size("grp").bit_length() - 1
    bits = [(b // (4 << i)) % 2 for i in reversed(range(line))] + [(b // 2) % 2]
    return bits + [(g // (1 << i)) % 2 for i in reversed(range(across))]


def steps_of(axis):
    line = (lax.axis_size("blk") // 4).bit_length() - 1
    across = lax.axis_size("grp").bit_length() - 1
    if axis == "y":
        return [(line, "blk", 2)]
    if axis == "x":
        return [(line + 1 + i, "grp", 1 << (across - 1 - i)) for i in range(across)]
    return [(line - 1 - axis, "blk", 4 << axis)] if axis < line else []


class PartSum:
    def __init__(self, send, keep, order):
        self.bits = place_bits()
        terms = [keep, lax.ppermute(send, "blk", swap("blk", 1))]
        self.terms = [t.reshape((2,) * len(self.bits) + (-1, t.shape[-1])) for t in terms]
        self.todo = [step for axis in orders(order) for step in steps_of(axis)]
        self.settled = []

    def sum(self, flip=None, token=0):
        total = 0.0
        for term in self.terms:
            at, sizes = [], []
            for dim, bit in enumerate(self.bits):
                pick = term.shape[dim] == 2 and dim in self.settled
                at.append((1 - bit if dim == flip else bit) + token if pick else 0)
                sizes.append(1 if pick else term.shape[dim])
            total = total + lax.dynamic_slice(
                term, (*at, 0, 0), (*sizes, *term.shape[-2:])
            ).astype(F32)
        return total

    def step(self, token=0):
        dim, axis, distance = self.todo.pop(0)
        self.settled.append(dim)
        sent = self.sum(dim, token).astype(BF)
        self.terms = self.terms + [lax.ppermute(sent, axis, swap(axis, distance))]
        return sent

    def before_last(self):
        *self.terms, _ = self.terms
        return self.sum().reshape(self.terms[0].shape[-2:])

    def result(self):
        while self.todo:
            self.step()
        return self.sum().reshape(self.terms[0].shape[-2:])


def joint_step(parts, token=0):
    dim, axis, distance = parts[0].todo[0]
    sent = []
    for part in parts:
        part.todo.pop(0)
        part.settled.append(dim)
        sent.append(part.sum(dim, token).astype(BF))
    sent = jnp.concatenate(sent, axis=-1)
    received = lax.ppermute(sent, axis, swap(axis, distance))
    at = 0
    for part in parts:
        width = part.terms[0].shape[-1]
        part.terms = part.terms + [received[..., at : at + width]]
        at += width
        part.last = received
    return sent


def advance(parts, token=0):
    if not parts[0].todo:
        return []
    if len(parts) > 1 and all(part.todo == parts[0].todo for part in parts):
        return [joint_step(parts, token)]
    return [part.step(token) for part in parts]


def finish(parts):
    received = parts[0].last.reshape(-1, parts[0].last.shape[-1])
    sums = [part.before_last() for part in parts]
    rows = received.shape[0]
    width = received.shape[1] - LANES

    def body(*refs):
        *sum_refs, last_ref, out, bias_one, bias_two = refs
        at = 0
        for ref in sum_refs:
            to = min(at + ref.shape[1], width)
            out[:, at:to] = ref[:, : to - at] + last_ref[:, at:to].astype(F32)
            at = to
        tile = (sum_refs[-1][:, -LANES:] + last_ref[:, width:].astype(F32)).T
        bias_one[...] = tile[:1]
        bias_two[...] = tile[LANES // 2 : LANES // 2 + 1]

    out, bias_one, bias_two = whole_call(
        body,
        [WHOLE] * (1 + len(sums)),
        [WHOLE] * 3,
        [sds((rows, width), F32), sds((1, rows), F32), sds((1, rows), F32)],
        flops=0,
    )(*sums, received)
    return out, [bias_one[0], bias_two[0]]


def orders(kind):
    rest = range(1, (lax.axis_size("blk") // 4).bit_length() - 1)
    return {
        "xyz": ["x", "y", 0, *rest],
        "yxz": ["y", "x", 0, *rest],
        "zxyz": [0, "x", "y", *rest],
        "xzyz": ["x", 0, "y", *rest],
        "yzxz": ["y", 0, "x", *rest],
        "zyxz": [0, "y", "x", *rest],
    }[kind]


def local(features, neighbours, degree, weight_one, bias_one, weight_two, bias_two, cotangent):
    core = (lax.axis_index("blk") % 2).reshape(1).astype(jnp.int32)
    inverse = 1.0 / (degree[0].astype(F32)[:, None] + 1.0)
    field = features[0]
    width = field.shape[1]

    near, far = field_halo(field)
    t_own, t_halo, n_own, n_halo, own = count_own(core, neighbours[0], degree[0], field)
    averaged_one, hidden, near, far, slope = layer(
        core, own, n_halo, near, far, inverse, weight_one, bias_one[None, :]
    )
    near, far = exchange(near, far)
    own = own_sum(n_own, hidden)
    averaged_two, activations, *halves = layer(
        core, own, n_halo, near, far, inverse, weight_two, bias_two[None, :], cotangent[0]
    )
    scaled, ends, _ = back_product(halves, weight_two, inverse, t_halo)
    near, far = exchange(ends[:BAND], ends[BAND:])

    *send, bias_a, bias_b = weight_half(core, averaged_two, halves, True)
    keep = weight_half(core, averaged_two, halves, False, None, send, 8)
    two = [PartSum(a, b, kind) for a, b, kind in zip(send, keep, ("xzyz","zxyz"))]
    sent = advance(two)

    grad_a, send_a, grad_bias_a = back_sum_weight(
        core, scaled, t_own, near, far, slope, averaged_one, 0, None, sent
    )
    grad_b, send_b, _, extra = back_sum_weight(
        core, scaled, t_own, near, far, slope, averaged_one, 1, [grad_bias_a, bias_a, bias_b]
    )
    keep = weight_half(core, averaged_one, [grad_a, grad_b], False, extra, [], 8)
    orders_one = ("yxz", "zxyz")
    one = [PartSum(s, k, order) for s, k, order in zip((send_a, send_b), keep, orders_one)]
    sent = advance(one) + advance(two)
    scaled, ends, token = back_product([grad_a, grad_b], weight_one, inverse, t_halo, sent)
    near, far = exchange(ends[:BAND], ends[BAND:])

    sent = advance(one, token[0])
    advance(two, token[0])
    advance(one)
    sent = advance(one)
    grad_input, token = back_sum(core, scaled, t_own, near, far, sent)
    while one[0].todo:
        advance(two, token[0])
        advance(one, token[0])
    grad_two = jnp.concatenate([part.result() for part in two], axis=1)
    grad_one, biases = finish(one)
    return activations[None], grad_input[None], grad_one, biases[0], grad_two, biases[1]


def solution(mesh):
    rows = P("grp", "blk", None)
    spread = ("blk", "grp")
    return jax.shard_map(
        local,
        mesh=mesh,
        in_specs=(rows, rows, P("grp", "blk"), P(), P(), P(), P(), rows),
        out_specs=(rows, rows, P(spread, None), P(spread), P(spread, None), P(spread)),
        check_vma=False,
    )
```
